32 devices in a mesh: dp: 2 (over x), ctx: 16 (over z, y, core).
Axes of the slice: x: 2, y: 2, z: 4, core: 2. Of those that a mesh axis runs over, the one named last changes fastest.
Arguments:
- queries: bfloat16 [4096, 2048], P(('dp', 'ctx')), parts along dimension 0, may hold values from -6 to 6
- keys: bfloat16 [4096, 2048], P(('dp', 'ctx')), parts along dimension 0, may hold values from -6 to 6
- values: bfloat16 [4096, 2048], P(('dp', 'ctx')), parts along dimension 0, may hold values from -6 to 6
- cotangent: bfloat16 [4096, 2048], P(('dp', 'ctx')), parts along dimension 0, may hold values from -6 to 6
- partner: int32 [16], P('dp'), parts along dimension 0, may hold values from 0 to 7, each once
Outputs:
- attended: bfloat16 [4096, 2048], P(('dp', 'ctx')), parts along dimension 0
- grad_queries: bfloat16 [4096, 2048], P(('dp', 'ctx')), parts along dimension 0
- grad_keys: bfloat16 [4096, 2048], P(('dp', 'ctx')), parts along dimension 0
- grad_values: bfloat16 [4096, 2048], P(('dp', 'ctx')), parts along dimension 0
The draws below stay inside these ranges and needn't reach their ends.
There are 2 independent parts, one for each index of `dp`. The reference program is written for one: setup_inputs(seed, part) draws one part's arguments, and reference() takes and returns one part's arrays. A program takes and returns all parts, laid end to end along the dimension named above; each array names one. Nothing has to cross between parts.
Inputs may be any that keep to these rules, and one draw needn't show every extreme that they name: `partner`: a permutation of the 8 block numbers.
All inputs are finite; a program needn't handle non-finite values.
Results may differ from the reference program's by a relative error of at most 0.012.
The reference program's roundings to bfloat16 on the way (of `coarse` and `grad_scores`) count: a program that leaves them out, or rounds other values in their place, can miss the bound.
Values may be sent and summed in bfloat16 or wider, within the bound.
No kernel may reach another device: no remote copies, remote signals or barrier semaphores. Data moves between devices by JAX's collectives and lax.ppermute only.
A program may use at most 128 MiB of HBM per device.

```python
import jax
import jax.numpy as jnp
from jax import lax

HEADS = 16
HEAD = 128
BLK = 256
SEQ = 2048
NB = 8
HW = 2048


def draw_queries(key, part):
    key = jax.random.fold_in(key, 17)
    background = jnp.clip(jax.random.normal(key, (SEQ, HEADS * HEAD)), -6.0, 6.0)
    return background.astype(jnp.bfloat16)


def draw_keys(key, part):
    key = jax.random.fold_in(key, 29)
    background = jnp.clip(jax.random.normal(key, (SEQ, HEADS * HEAD)), -6.0, 6.0)
    return background.astype(jnp.bfloat16)


def level_of(rng, shape, cuts, smallest, high):
    def one(dim, blocks):
        heights = jax.random.uniform(jax.random.fold_in(jax.random.fold_in(rng, 6), dim), (blocks,), jnp.float32, smallest / len(cuts), high / len(cuts))
        return jnp.repeat(jnp.exp(heights), shape[dim] // blocks).reshape((-1,) + (1,) * (len(shape) - dim - 1))

    level = one(*cuts[0])
    for cut in cuts[1:]:
        level = level * one(*cut)
    return level


def centred(stream_key, shape, width, reach, cuts=(), held_as=jnp.bfloat16):
    result = width * jax.random.normal(stream_key, shape, jnp.float32)
    if cuts:
        result = result * level_of(stream_key, shape, cuts, -0.22, 0.18)
    return jnp.clip(result, -reach, reach).astype(held_as)


def setup_inputs(seed: int = 0, part: int = 0) -> dict:
    key_of = jax.random.split(jax.random.key(seed), 6)
    part_keys = jax.random.split(jax.random.fold_in(key_of[5], part), 6)
    queries = draw_queries(jax.random.fold_in(jax.random.fold_in(key_of[5], part), 71), part)
    keys = draw_keys(jax.random.fold_in(jax.random.fold_in(key_of[5], part), 71), part)
    values = centred(part_keys[2], (SEQ, HW), 1.0, 6.0, ((0, 16),))
    cotangent = centred(part_keys[3], (SEQ, HW), 1.0, 6.0, ((0, 16),))
    partner = jax.random.permutation(part_keys[4], NB).astype(jnp.int32)
    return dict(queries=queries, keys=keys, values=values, cotangent=cotangent, partner=partner)


def attend(query_heads, key_heads, value_heads, grad_heads):
    scale_factor = HEAD ** -0.5
    scores = jnp.einsum('qhd,khd->hqk', query_heads, key_heads, preferred_element_type=jnp.float32) * scale_factor
    row_peak = jnp.max(scores, axis=2, keepdims=True)
    exponent = jnp.exp(scores - row_peak)
    row_total = jnp.sum(exponent, axis=2, keepdims=True)
    weights = exponent / row_total
    coarse = weights.astype(jnp.bfloat16)
    attended_part = jnp.einsum('hqk,khd->qhd', coarse, value_heads, preferred_element_type=jnp.float32).astype(jnp.bfloat16)
    stored = lax.optimization_barrier(attended_part)
    row_delta = jnp.sum(grad_heads.astype(jnp.float32) * stored.astype(jnp.float32), axis=2)
    grad_weights = jnp.einsum('qhd,khd->hqk', grad_heads, value_heads, preferred_element_type=jnp.float32)
    grad_scores = (weights * (grad_weights - row_delta.T[:, :, None])).astype(jnp.bfloat16)
    grad_query_part = (scale_factor * jnp.einsum('hqk,khd->qhd', grad_scores, key_heads, preferred_element_type=jnp.float32)).astype(jnp.bfloat16)
    key_terms = scale_factor * jnp.einsum('hqk,qhd->khd', grad_scores, query_heads, preferred_element_type=jnp.float32)
    value_terms = jnp.einsum('hqk,qhd->khd', coarse, grad_heads, preferred_element_type=jnp.float32)
    return attended_part, grad_query_part, key_terms, value_terms


def reference(queries, keys, values, cotangent, partner):
    def one_block(block_index):
        own_start = (block_index * BLK).astype(jnp.int32)
        far_start = (lax.dynamic_index_in_dim(partner, block_index, keepdims=False) * BLK).astype(jnp.int32)

        def block_rows(source_array, row_start):
            return lax.dynamic_slice_in_dim(source_array, row_start, BLK, 0)

        query_heads = block_rows(queries, own_start).reshape(BLK, HEADS, HEAD)
        grad_heads = block_rows(cotangent, own_start).reshape(BLK, HEADS, HEAD)
        key_heads = jnp.concatenate([block_rows(keys, own_start), block_rows(keys, far_start)], axis=0).reshape(2 * BLK, HEADS, HEAD)
        value_heads = jnp.concatenate([block_rows(values, own_start), block_rows(values, far_start)], axis=0).reshape(2 * BLK, HEADS, HEAD)
        attended_part, grad_query_part, key_terms, value_terms = attend(query_heads, key_heads, value_heads, grad_heads)
        return (attended_part.reshape(BLK, HW), grad_query_part.reshape(BLK, HW),
                key_terms.reshape(2 * BLK, HW), value_terms.reshape(2 * BLK, HW))

    results = lax.map(one_block, jnp.arange(NB, dtype=jnp.int32))
    attended = results[0].reshape(SEQ, HW)
    grad_queries = results[1].reshape(SEQ, HW)

    def collect(term_table):
        partner_terms = jnp.zeros_like(term_table[:, BLK:]).at[partner].add(term_table[:, BLK:])
        return (term_table[:, :BLK] + partner_terms).reshape(SEQ, HW).astype(jnp.bfloat16)

    return attended, grad_queries, collect(results[2]), collect(results[3])
```

```python
import functools

import jax
import jax.numpy as jnp
from jax import lax
from jax.experimental import pallas as pl
from jax.experimental.pallas import tpu as pltpu
from jax.sharding import PartitionSpec as P

HEAD = 128
SCALE = HEAD ** (-0.5)

NN = (((1,), (0,)), ((), ()))
NT = (((1,), (1,)), ((), ()))
TN = (((0,), (0,)), ((), ()))


def mm(a, b, dims):
    return lax.dot_general(a, b, dims, preferred_element_type=jnp.float32)


def attention_kernel(pieces, blocks, first, partner, local, far, out, grad_k, grad_v, acc_k, acc_v):
    per_block = pieces // blocks
    block_rows = per_block * local.shape[2]
    total_blocks = acc_k.shape[0]

    def rows(ref, piece, which):
        return ref[pl.ds(piece * per_block, per_block), which].reshape(block_rows, HEAD)

    acc_k[...] = jnp.zeros_like(acc_k)
    acc_v[...] = jnp.zeros_like(acc_v)

    def one(b, carry):
        own = first[0] + b
        p = partner[own]
        q = rows(local, b, 0)
        do = rows(local, b, 3)
        ks, vs = [rows(local, b, 1)], [rows(local, b, 2)]
        if far is None:
            ks.append(rows(local, p, 1))
            vs.append(rows(local, p, 2))
        else:
            ks.append(rows(far, p, 0))
            vs.append(rows(far, p, 1))
        scores = [mm(q, k, NT) * SCALE for k in ks]
        peak = jnp.max(jnp.maximum(scores[0], scores[1]), axis=1, keepdims=True)
        exps = [jnp.exp(s - peak) for s in scores]
        total = jnp.sum(exps[0] + exps[1], axis=1, keepdims=True)
        inverse = 1.0 / total
        weights = [e * inverse for e in exps]
        coarse = [w.astype(jnp.bfloat16) for w in weights]
        attended = (mm(coarse[0], vs[0], NN) + mm(coarse[1], vs[1], NN)).astype(jnp.bfloat16)
        delta = jnp.sum(
            do.astype(jnp.float32) * attended.astype(jnp.float32), axis=1, keepdims=True
        )
        gs = [
            (w * (mm(do, v, NT) - delta)).astype(jnp.bfloat16) for w, v in zip(weights, vs)
        ]
        grad_q = (SCALE * (mm(gs[0], ks[0], NN) + mm(gs[1], ks[1], NN))).astype(jnp.bfloat16)
        here = pl.ds(b * per_block, per_block)
        out[here, 0] = attended.reshape(per_block, -1, HEAD)
        out[here, 1] = grad_q.reshape(per_block, -1, HEAD)
        for target, g, c in zip((own, p), gs, coarse):
            acc_k[target] += SCALE * mm(g, q, TN)
            acc_v[target] += mm(c, do, TN)
        return carry

    lax.fori_loop(0, blocks, one, 0)
    if grad_k is None:
        for which, acc in ((2, acc_k), (3, acc_v)):
            out[:, which] = acc[...].reshape(pieces, -1, HEAD).astype(jnp.bfloat16)
    else:
        grad_k[...] = acc_k[...]
        grad_v[...] = acc_v[...]


def attention(partner, first, local, far, blocks):
    pieces, _, rows, _ = local.shape
    total_blocks = partner.shape[0]
    block_rows = pieces // blocks * rows
    whole = far is None
    smem = pl.BlockSpec(memory_space=pltpu.SMEM)
    vmem = pl.BlockSpec(memory_space=pltpu.VMEM)
    grads = jax.ShapeDtypeStruct((total_blocks, block_rows, HEAD), jnp.float32)
    out_shape = [jax.ShapeDtypeStruct((pieces, 4 if whole else 2, rows, HEAD), jnp.bfloat16)]
    operands = [first, partner, local]
    if not whole:
        out_shape += [grads, grads]
        operands.append(far)

    def kernel(*refs):
        n = len(operands)
        m = n + len(out_shape)
        ins, outs, scratch = refs[:n], refs[n:m], refs[m:]
        attention_kernel(
            pieces,
            blocks,
            ins[0],
            ins[1],
            ins[2],
            None if whole else ins[3],
            outs[0],
            None if whole else outs[1],
            None if whole else outs[2],
            *scratch,
        )

    flops = 12 * blocks * block_rows * 2 * block_rows * HEAD
    return pl.pallas_call(
        kernel,
        out_shape=out_shape,
        in_specs=[smem, smem] + [vmem] * (len(operands) - 2),
        out_specs=[vmem] * len(out_shape),
        scratch_shapes=[pltpu.VMEM((total_blocks, block_rows, HEAD), jnp.float32)] * 2,
        compiler_params=pltpu.CompilerParams(vmem_limit_bytes=48 * 1024 * 1024),
        cost_estimate=pl.CostEstimate(
            flops=flops,
            bytes_accessed=2 * local.size * 2,
            transcendentals=blocks * block_rows * 2 * block_rows,
        ),
    )(*operands)


def body(queries, keys, values, cotangent, partner):
    rows, width = queries.shape
    devices = lax.axis_size("ctx")
    heads = width // HEAD
    blocks = partner.shape[0]
    spread = min(heads, devices)
    groups = devices // spread
    heads_here = heads // spread
    near = [[g * spread + i for i in range(spread)] for g in range(groups)]
    across = [[g * spread + i for g in range(groups)] for i in range(spread)]
    group = lax.axis_index("ctx") // spread
    exchange = functools.partial(
        lax.all_to_all,
        axis_name="ctx",
        split_axis=0,
        concat_axis=0,
        tiled=True,
        axis_index_groups=near if groups > 1 else None,
    )

    def pack(arrays):
        stacked = jnp.stack(arrays).reshape(len(arrays), rows, spread, heads_here, HEAD)
        return stacked.transpose(2, 3, 0, 1, 4)

    def unpack(packed):
        kinds = packed.shape[2]
        full = packed.transpose(2, 3, 0, 1, 4).reshape(kinds, rows, width)
        return [full[i] for i in range(kinds)]

    local_blocks = blocks // groups
    first = (group * local_blocks).astype(jnp.int32).reshape(1)
    local = exchange(pack([queries, keys, values, cotangent]))
    outs = []
    for h in range(heads_here):
        mine = local[:, h]
        if groups == 1:
            outs.append(attention(partner, first, mine, None, local_blocks)[0])
        else:
            far = lax.all_gather(
                mine[:, 1:3], "ctx", axis=0, tiled=True, axis_index_groups=across
            )
            out, grad_k, grad_v = attention(partner, first, mine, far, local_blocks)
            grads = lax.psum_scatter(
                jnp.stack([grad_k, grad_v], axis=1),
                "ctx",
                scatter_dimension=0,
                tiled=True,
                axis_index_groups=across,
            ).astype(jnp.bfloat16)
            grads = grads.transpose(0, 2, 1, 3).reshape(spread, rows, 2, HEAD).transpose(0, 2, 1, 3)
            outs.append(jnp.concatenate([out, grads], axis=1))
    return tuple(unpack(exchange(jnp.stack(outs, axis=1))))


def solution(mesh):
    split = P(("dp", "ctx"), None)
    return jax.shard_map(
        body,
        mesh=mesh,
        in_specs=(split, split, split, split, P("dp")),
        out_specs=(split, split, split, split),
        check_vma=False,
    )
```

```python
import functools

import jax
import jax.numpy as jnp
from jax import lax
from jax.experimental import pallas as pl
from jax.experimental.pallas import tpu as pltpu
from jax.sharding import PartitionSpec as P

HEAD = 128
SCALE = HEAD ** (-0.5)

NN = (((1,), (0,)), ((), ()))
NT = (((1,), (1,)), ((), ()))
TN = (((0,), (0,)), ((), ()))


def mm(a, b, dims):
    return lax.dot_general(a, b, dims, preferred_element_type=jnp.float32)


def attention_kernel(pieces, blocks, first, partner, local, far, out, grad_k, grad_v, acc_k, acc_v):
    per_block = pieces // blocks
    block_rows = per_block * local.shape[2]
    total_blocks = acc_k.shape[0]

    def rows(ref, piece, which):
        return ref[pl.ds(piece * per_block, per_block), which].reshape(block_rows, HEAD)

    acc_k[...] = jnp.zeros_like(acc_k)
    acc_v[...] = jnp.zeros_like(acc_v)

    def one(b, carry):
        own = first[0] + b
        p = partner[own]
        q = rows(local, b, 0)
        do = rows(local, b, 3)
        ks, vs = [rows(local, b, 1)], [rows(local, b, 2)]
        if far is None:
            ks.append(rows(local, p, 1))
            vs.append(rows(local, p, 2))
        else:
            ks.append(rows(far, p, 0))
            vs.append(rows(far, p, 1))
        scores = [mm(q, k, NT) * SCALE for k in ks]
        peak = jnp.max(jnp.maximum(scores[0], scores[1]), axis=1, keepdims=True)
        exps = [jnp.exp(s - peak) for s in scores]
        total = jnp.sum(exps[0] + exps[1], axis=1, keepdims=True)
        inverse = 1.0 / total
        weights = [e * inverse for e in exps]
        coarse = [w.astype(jnp.bfloat16) for w in weights]
        attended = (mm(coarse[0], vs[0], NN) + mm(coarse[1], vs[1], NN)).astype(jnp.bfloat16)
        delta = jnp.sum(
            do.astype(jnp.float32) * attended.astype(jnp.float32), axis=1, keepdims=True
        )
        gs = [
            (w * (mm(do, v, NT) - delta)).astype(jnp.bfloat16) for w, v in zip(weights, vs)
        ]
        grad_q = (SCALE * (mm(gs[0], ks[0], NN) + mm(gs[1], ks[1], NN))).astype(jnp.bfloat16)
        here = pl.ds(b * per_block, per_block)
        out[here, 0] = attended.reshape(per_block, -1, HEAD)
        out[here, 1] = grad_q.reshape(per_block, -1, HEAD)
        for target, g, c in zip((own, p), gs, coarse):
            acc_k[target] += SCALE * mm(g, q, TN)
            acc_v[target] += mm(c, do, TN)
        return carry

    lax.fori_loop(0, blocks, one, 0)
    if grad_k is None:
        for which, acc in ((2, acc_k), (3, acc_v)):
            out[:, which] = acc[...].reshape(pieces, -1, HEAD).astype(jnp.bfloat16)
    else:
        grad_k[...] = acc_k[...]
        grad_v[...] = acc_v[...]


def attention(partner, first, local, far, blocks):
    pieces, _, rows, _ = local.shape
    total_blocks = partner.shape[0]
    block_rows = pieces // blocks * rows
    whole = far is None
    smem = pl.BlockSpec(memory_space=pltpu.SMEM)
    vmem = pl.BlockSpec(memory_space=pltpu.VMEM)
    grads = jax.ShapeDtypeStruct((total_blocks, block_rows, HEAD), jnp.float32)
    out_shape = [jax.ShapeDtypeStruct((pieces, 4 if whole else 2, rows, HEAD), jnp.bfloat16)]
    operands = [first, partner, local]
    if not whole:
        out_shape += [grads, grads]
        operands.append(far)

    def kernel(*refs):
        n = len(operands)
        m = n + len(out_shape)
        ins, outs, scratch = refs[:n], refs[n:m], refs[m:]
        attention_kernel(
            pieces,
            blocks,
            ins[0],
            ins[1],
            ins[2],
            None if whole else ins[3],
            outs[0],
            None if whole else outs[1],
            None if whole else outs[2],
            *scratch,
        )

    flops = 12 * blocks * block_rows * 2 * block_rows * HEAD
    return pl.pallas_call(
        kernel,
        out_shape=out_shape,
        in_specs=[smem, smem] + [vmem] * (len(operands) - 2),
        out_specs=[vmem] * len(out_shape),
        scratch_shapes=[pltpu.VMEM((total_blocks, block_rows, HEAD), jnp.float32)] * 2,
        compiler_params=pltpu.CompilerParams(vmem_limit_bytes=48 * 1024 * 1024),
        cost_estimate=pl.CostEstimate(
            flops=flops,
            bytes_accessed=2 * local.size * 2,
            transcendentals=blocks * block_rows * 2 * block_rows,
        ),
    )(*operands)


def by_all_to_all(queries, keys, values, cotangent, partner):
    rows, width = queries.shape
    devices = lax.axis_size("ctx")
    heads = width // HEAD
    blocks = partner.shape[0]
    spread = min(heads, devices)
    groups = devices // spread
    heads_here = heads // spread
    near = [[g * spread + i for i in range(spread)] for g in range(groups)]
    across = [[g * spread + i for g in range(groups)] for i in range(spread)]
    group = lax.axis_index("ctx") // spread
    exchange = functools.partial(
        lax.all_to_all,
        axis_name="ctx",
        split_axis=0,
        concat_axis=0,
        tiled=True,
        axis_index_groups=near if groups > 1 else None,
    )

    def pack(arrays):
        stacked = jnp.stack(arrays).reshape(len(arrays), rows, spread, heads_here, HEAD)
        return stacked.transpose(2, 3, 0, 1, 4)

    def unpack(packed):
        kinds = packed.shape[2]
        full = packed.transpose(2, 3, 0, 1, 4).reshape(kinds, rows, width)
        return [full[i] for i in range(kinds)]

    local_blocks = blocks // groups
    first = (group * local_blocks).astype(jnp.int32).reshape(1)
    local = exchange(pack([queries, keys, values, cotangent]))
    outs = []
    for h in range(heads_here):
        mine = local[:, h]
        if groups == 1:
            outs.append(attention(partner, first, mine, None, local_blocks)[0])
        else:
            far = lax.all_gather(
                mine[:, 1:3], "ctx", axis=0, tiled=True, axis_index_groups=across
            )
            out, grad_k, grad_v = attention(partner, first, mine, far, local_blocks)
            grads = lax.psum_scatter(
                jnp.stack([grad_k, grad_v], axis=1),
                "ctx",
                scatter_dimension=0,
                tiled=True,
                axis_index_groups=across,
            ).astype(jnp.bfloat16)
            grads = grads.transpose(0, 2, 1, 3).reshape(spread, rows, 2, HEAD).transpose(0, 2, 1, 3)
            outs.append(jnp.concatenate([out, grads], axis=1))
    return tuple(unpack(exchange(jnp.stack(outs, axis=1))))


def call(kernel, place, arrays, out_shape, scratch=(), flops=0, exps=0):
    smem = pl.BlockSpec(memory_space=pltpu.SMEM)
    vmem = pl.BlockSpec(memory_space=pltpu.VMEM)
    moved = sum(a.size * a.dtype.itemsize for a in arrays)
    moved += sum(a.size * a.dtype.itemsize for a in out_shape)
    return pl.pallas_call(
        kernel,
        out_shape=out_shape,
        in_specs=[smem] * len(place) + [vmem] * len(arrays),
        out_specs=[vmem] * len(out_shape),
        scratch_shapes=list(scratch),
        compiler_params=pltpu.CompilerParams(vmem_limit_bytes=40 * 1024 * 1024),
        cost_estimate=pl.CostEstimate(flops=flops, bytes_accessed=moved, transcendentals=exps),
    )(*place, *arrays)


def pack(place, arrays, chips):
    count = len(arrays)
    rows, width = arrays[0].shape
    span = width // chips

    def kernel(where, *refs):
        for k in range(chips):
            start = pl.multiple_of((where[0] ^ k) * span, span)
            for i in range(count):
                refs[count + k][i] = refs[i][:, pl.ds(start, span)]

    piece = jax.ShapeDtypeStruct((count, rows, span), jnp.bfloat16)
    return call(kernel, [place], arrays, [piece] * chips)


def unpack(place, mine, theirs):
    chips = len(mine)
    count, both, head = mine[0].shape
    rows = both // 2

    def kernel(where, *refs):
        core = where[1]
        half = pl.ds(pl.multiple_of(core * rows, rows), rows)
        for k in range(chips):
            start = (where[0] ^ k) * 2
            here = pl.multiple_of((start + core) * head, head)
            there = pl.multiple_of((start + 1 - core) * head, head)
            for i in range(count):
                out = refs[2 * chips + i]
                out[:, pl.ds(here, head)] = refs[k][i, half]
                out[:, pl.ds(there, head)] = refs[chips + k][i, half]

    out = jax.ShapeDtypeStruct((rows, chips * 2 * head), jnp.bfloat16)
    return call(kernel, [place], [*mine, *theirs], [out] * count)


def merge(where, mine, theirs, target):
    core = where[1]
    rows = mine[0].shape[1]
    column = pl.ds(pl.multiple_of(core * HEAD, HEAD), HEAD)
    here = pl.ds(pl.multiple_of(core * rows, rows), rows)
    there = pl.ds(pl.multiple_of((1 - core) * rows, rows), rows)
    for k in range(len(mine)):
        block = where[0] ^ k
        for i in range(mine[0].shape[0]):
            target[block, i, here] = mine[k][i, :, column]
            target[block, i, there] = theirs[k][i, :, column]


def forward(place, partner, mine, theirs):
    chips = len(mine)
    size = 2 * mine[0].shape[1]

    def kernel(where, partner, *refs):
        ins, outs = refs[: 2 * chips], refs[2 * chips :]
        held, weights = outs[chips], outs[chips + 1]
        merge(where, ins[:chips], ins[chips:], held)
        for k in range(chips):
            b = where[0] ^ k
            p = partner[b]
            q = held[b, 0]
            s = mm(q, held[b, 1], NT) * SCALE
            t = mm(q, held[p, 1], NT) * SCALE
            peak = jnp.max(jnp.maximum(s, t), axis=1, keepdims=True)
            s, t = jnp.exp(s - peak), jnp.exp(t - peak)
            inverse = 1.0 / jnp.sum(s + t, axis=1, keepdims=True)
            s, t = s * inverse, t * inverse
            weights[b, 0] = s
            weights[b, 1] = t
            attended = mm(s.astype(jnp.bfloat16), held[b, 2], NN)
            attended += mm(t.astype(jnp.bfloat16), held[p, 2], NN)
            attended = attended.astype(jnp.bfloat16)
            outs[k][0] = attended
            held[b, 3] = attended

    out_shape = [jax.ShapeDtypeStruct((1, size, HEAD), jnp.bfloat16)] * chips
    out_shape += [
        jax.ShapeDtypeStruct((chips, 4, size, HEAD), jnp.bfloat16),
        jax.ShapeDtypeStruct((chips, 2, size, size), jnp.float32),
    ]
    flops = chips * 8 * size * size * HEAD
    outs = call(
        kernel, [place, partner], [*mine, *theirs], out_shape, (), flops, chips * 2 * size * size
    )
    return outs[:chips], outs[chips], outs[chips + 1]


def backward(place, partner, mine, theirs, held, weights):
    chips = len(mine)
    size = held.shape[2]

    def kernel(where, partner, *refs):
        ins, outs = refs[: 2 * chips + 2], refs[2 * chips + 2 : 3 * chips + 2]
        held, weights = ins[2 * chips :]
        grads, acc_k, acc_v = refs[3 * chips + 2 :]
        merge(where, ins[:chips], ins[chips : 2 * chips], grads)
        acc_k[...] = jnp.zeros_like(acc_k)
        acc_v[...] = jnp.zeros_like(acc_v)
        for k in range(chips):
            b = where[0] ^ k
            q, do = held[b, 0], grads[b, 0]
            delta = jnp.sum(
                do.astype(jnp.float32) * held[b, 3].astype(jnp.float32), axis=1, keepdims=True
            )
            grad_q = None
            for side, c in enumerate((b, partner[b])):
                w = weights[b, side]
                g = (w * (mm(do, held[c, 2], NT) - delta)).astype(jnp.bfloat16)
                term = mm(g, held[c, 1], NN)
                grad_q = term if side == 0 else grad_q + term
                acc_k[c] += mm(g, q, TN)
                acc_v[c] += mm(w.astype(jnp.bfloat16), do, TN)
            outs[k][0] = (SCALE * grad_q).astype(jnp.bfloat16)
        for k in range(chips):
            b = where[0] ^ k
            outs[k][1] = (SCALE * acc_k[b]).astype(jnp.bfloat16)
            outs[k][2] = acc_v[b].astype(jnp.bfloat16)

    out_shape = [jax.ShapeDtypeStruct((3, size, HEAD), jnp.bfloat16)] * chips
    scratch = [
        pltpu.VMEM((chips, 1, size, HEAD), jnp.bfloat16),
        pltpu.VMEM((chips, size, HEAD), jnp.float32),
        pltpu.VMEM((chips, size, HEAD), jnp.float32),
    ]
    flops = chips * 16 * size * size * HEAD
    return call(
        kernel, [place, partner], [*mine, *theirs, held, weights], out_shape, scratch, flops
    )


def between_chips(pieces):
    devices = 2 * len(pieces)
    return [
        lax.ppermute(p, "ctx", [(i, i ^ (2 * k)) for i in range(devices)]) if k else p
        for k, p in enumerate(pieces)
    ]


def between_cores(pieces):
    devices = 2 * len(pieces)
    return [lax.ppermute(p, "ctx", [(i, i ^ 1) for i in range(devices)]) for p in pieces]


def by_permutes(queries, keys, values, cotangent, partner):
    chips = lax.axis_size("ctx") // 2
    me = lax.axis_index("ctx")
    place = jnp.stack([me // 2, me % 2]).astype(jnp.int32)
    first = between_chips(pack(place, [queries, keys, values], chips))
    second = between_chips(pack(place, [cotangent], chips))
    attended, held, weights = forward(place, partner, first, between_cores(first))
    grads = backward(place, partner, second, between_cores(second), held, weights)
    attended = between_chips(attended)
    outs = unpack(place, attended, between_cores(attended))
    grads = between_chips(grads)
    return tuple(outs) + tuple(unpack(place, grads, between_cores(grads)))


def body(queries, keys, values, cotangent, partner):
    rows, width = queries.shape
    devices = lax.axis_size("ctx")
    blocks = partner.shape[0]
    in_pairs = devices == 2 * blocks and devices * HEAD == width
    if in_pairs and blocks & (blocks - 1) == 0:
        return by_permutes(queries, keys, values, cotangent, partner)
    return by_all_to_all(queries, keys, values, cotangent, partner)


def solution(mesh):
    split = P(("dp", "ctx"), None)
    return jax.shard_map(
        body,
        mesh=mesh,
        in_specs=(split, split, split, split, P("dp")),
        out_specs=(split, split, split, split),
        check_vma=False,
    )
```

```python
import functools

import jax
import jax.numpy as jnp
from jax import lax
from jax.experimental import pallas as pl
from jax.experimental.pallas import tpu as pltpu
from jax.sharding import PartitionSpec as P

HEAD = 128
SCALE = HEAD ** (-0.5)

NN = (((1,), (0,)), ((), ()))
NT = (((1,), (1,)), ((), ()))
TN = (((0,), (0,)), ((), ()))


def mm(a, b, dims):
    return lax.dot_general(a, b, dims, preferred_element_type=jnp.float32)


def attention_kernel(pieces, blocks, first, partner, local, far, out, grad_k, grad_v, acc_k, acc_v):
    per_block = pieces // blocks
    block_rows = per_block * local.shape[2]
    total_blocks = acc_k.shape[0]

    def rows(ref, piece, which):
        return ref[pl.ds(piece * per_block, per_block), which].reshape(block_rows, HEAD)

    acc_k[...] = jnp.zeros_like(acc_k)
    acc_v[...] = jnp.zeros_like(acc_v)

    def one(b, carry):
        own = first[0] + b
        p = partner[own]
        q = rows(local, b, 0)
        do = rows(local, b, 3)
        ks, vs = [rows(local, b, 1)], [rows(local, b, 2)]
        if far is None:
            ks.append(rows(local, p, 1))
            vs.append(rows(local, p, 2))
        else:
            ks.append(rows(far, p, 0))
            vs.append(rows(far, p, 1))
        scores = [mm(q, k, NT) * SCALE for k in ks]
        peak = jnp.max(jnp.maximum(scores[0], scores[1]), axis=1, keepdims=True)
        exps = [jnp.exp(s - peak) for s in scores]
        total = jnp.sum(exps[0] + exps[1], axis=1, keepdims=True)
        inverse = 1.0 / total
        weights = [e * inverse for e in exps]
        coarse = [w.astype(jnp.bfloat16) for w in weights]
        attended = (mm(coarse[0], vs[0], NN) + mm(coarse[1], vs[1], NN)).astype(jnp.bfloat16)
        delta = jnp.sum(
            do.astype(jnp.float32) * attended.astype(jnp.float32), axis=1, keepdims=True
        )
        gs = [
            (w * (mm(do, v, NT) - delta)).astype(jnp.bfloat16) for w, v in zip(weights, vs)
        ]
        grad_q = (SCALE * (mm(gs[0], ks[0], NN) + mm(gs[1], ks[1], NN))).astype(jnp.bfloat16)
        here = pl.ds(b * per_block, per_block)
        out[here, 0] = attended.reshape(per_block, -1, HEAD)
        out[here, 1] = grad_q.reshape(per_block, -1, HEAD)
        for target, g, c in zip((own, p), gs, coarse):
            acc_k[target] += SCALE * mm(g, q, TN)
            acc_v[target] += mm(c, do, TN)
        return carry

    lax.fori_loop(0, blocks, one, 0)
    if grad_k is None:
        for which, acc in ((2, acc_k), (3, acc_v)):
            out[:, which] = acc[...].reshape(pieces, -1, HEAD).astype(jnp.bfloat16)
    else:
        grad_k[...] = acc_k[...]
        grad_v[...] = acc_v[...]


def attention(partner, first, local, far, blocks):
    pieces, _, rows, _ = local.shape
    total_blocks = partner.shape[0]
    block_rows = pieces // blocks * rows
    whole = far is None
    smem = pl.BlockSpec(memory_space=pltpu.SMEM)
    vmem = pl.BlockSpec(memory_space=pltpu.VMEM)
    grads = jax.ShapeDtypeStruct((total_blocks, block_rows, HEAD), jnp.float32)
    out_shape = [jax.ShapeDtypeStruct((pieces, 4 if whole else 2, rows, HEAD), jnp.bfloat16)]
    operands = [first, partner, local]
    if not whole:
        out_shape += [grads, grads]
        operands.append(far)

    def kernel(*refs):
        n = len(operands)
        m = n + len(out_shape)
        ins, outs, scratch = refs[:n], refs[n:m], refs[m:]
        attention_kernel(
            pieces,
            blocks,
            ins[0],
            ins[1],
            ins[2],
            None if whole else ins[3],
            outs[0],
            None if whole else outs[1],
            None if whole else outs[2],
            *scratch,
        )

    flops = 12 * blocks * block_rows * 2 * block_rows * HEAD
    return pl.pallas_call(
        kernel,
        out_shape=out_shape,
        in_specs=[smem, smem] + [vmem] * (len(operands) - 2),
        out_specs=[vmem] * len(out_shape),
        scratch_shapes=[pltpu.VMEM((total_blocks, block_rows, HEAD), jnp.float32)] * 2,
        compiler_params=pltpu.CompilerParams(vmem_limit_bytes=48 * 1024 * 1024),
        cost_estimate=pl.CostEstimate(
            flops=flops,
            bytes_accessed=2 * local.size * 2,
            transcendentals=blocks * block_rows * 2 * block_rows,
        ),
    )(*operands)


def by_all_to_all(queries, keys, values, cotangent, partner):
    rows, width = queries.shape
    devices = lax.axis_size("ctx")
    heads = width // HEAD
    blocks = partner.shape[0]
    spread = min(heads, devices)
    groups = devices // spread
    heads_here = heads // spread
    near = [[g * spread + i for i in range(spread)] for g in range(groups)]
    across = [[g * spread + i for g in range(groups)] for i in range(spread)]
    group = lax.axis_index("ctx") // spread
    exchange = functools.partial(
        lax.all_to_all,
        axis_name="ctx",
        split_axis=0,
        concat_axis=0,
        tiled=True,
        axis_index_groups=near if groups > 1 else None,
    )

    def pack(arrays):
        stacked = jnp.stack(arrays).reshape(len(arrays), rows, spread, heads_here, HEAD)
        return stacked.transpose(2, 3, 0, 1, 4)

    def unpack(packed):
        kinds = packed.shape[2]
        full = packed.transpose(2, 3, 0, 1, 4).reshape(kinds, rows, width)
        return [full[i] for i in range(kinds)]

    local_blocks = blocks // groups
    first = (group * local_blocks).astype(jnp.int32).reshape(1)
    local = exchange(pack([queries, keys, values, cotangent]))
    outs = []
    for h in range(heads_here):
        mine = local[:, h]
        if groups == 1:
            outs.append(attention(partner, first, mine, None, local_blocks)[0])
        else:
            far = lax.all_gather(
                mine[:, 1:3], "ctx", axis=0, tiled=True, axis_index_groups=across
            )
            out, grad_k, grad_v = attention(partner, first, mine, far, local_blocks)
            grads = lax.psum_scatter(
                jnp.stack([grad_k, grad_v], axis=1),
                "ctx",
                scatter_dimension=0,
                tiled=True,
                axis_index_groups=across,
            ).astype(jnp.bfloat16)
            grads = grads.transpose(0, 2, 1, 3).reshape(spread, rows, 2, HEAD).transpose(0, 2, 1, 3)
            outs.append(jnp.concatenate([out, grads], axis=1))
    return tuple(unpack(exchange(jnp.stack(outs, axis=1))))


def call(kernel, place, arrays, out_shape, scratch=(), flops=0, exps=0, in_place=0):
    smem = pl.BlockSpec(memory_space=pltpu.SMEM)
    vmem = pl.BlockSpec(memory_space=pltpu.VMEM)
    moved = sum(a.size * a.dtype.itemsize for a in arrays)
    moved += sum(a.size * a.dtype.itemsize for a in out_shape)
    return pl.pallas_call(
        kernel,
        out_shape=out_shape,
        in_specs=[smem] * len(place)
        + [pl.BlockSpec(memory_space=pltpu.HBM)] * in_place
        + [vmem] * (len(arrays) - in_place),
        out_specs=[vmem] * len(out_shape),
        scratch_shapes=list(scratch),
        compiler_params=pltpu.CompilerParams(vmem_limit_bytes=40 * 1024 * 1024),
        cost_estimate=pl.CostEstimate(flops=flops, bytes_accessed=moved, transcendentals=exps),
    )(*place, *arrays)


def pack(place, mine, theirs, chips):
    count = len(mine)
    rows, width = mine[0].shape

    def kernel(where, *refs):
        mine, theirs = refs[:count], refs[count : 2 * count]
        outs, sems = refs[2 * count : -1], refs[-1]
        here, there = halves(where, rows)
        column = [
            pl.ds(pl.multiple_of(((where[0] ^ k) * 2 + where[1]) * HEAD, HEAD), HEAD)
            for k in range(chips)
        ]
        copies = [
            pltpu.make_async_copy(mine[i].at[:, column[k]], outs[k].at[i, here], sems.at[k, i])
            for k in range(chips)
            for i in range(count)
        ]
        for copy in copies:
            copy.start()
        for k in range(chips):
            for i in range(count):
                outs[k][i, there] = theirs[i][:, column[k]]
        for copy in copies:
            copy.wait()

    piece = jax.ShapeDtypeStruct((count, 2 * rows, HEAD), jnp.bfloat16)
    return call(
        kernel,
        [place],
        [*mine, *theirs],
        [piece] * chips,
        [pltpu.SemaphoreType.DMA((chips, count))],
        in_place=count,
    )


def pair(place, keep, got):
    chips, count, rows, _ = keep.shape

    def kernel(where, keep, got, *outs):
        core = where[1]
        here = pl.ds(pl.multiple_of(core * HEAD, HEAD), HEAD)
        there = pl.ds(pl.multiple_of((1 - core) * HEAD, HEAD), HEAD)
        for k in range(chips):
            for i in range(count):
                outs[k][i, :, here] = keep[k, i]
                outs[k][i, :, there] = got[k, i]

    piece = jax.ShapeDtypeStruct((count, rows, 2 * HEAD), jnp.bfloat16)
    return call(kernel, [place], [keep, got], [piece] * chips)


def unpack(place, ks, pieces):
    chips = len(pieces)
    count, rows, span = pieces[0].shape

    def kernel(where, *refs):
        for n, k in enumerate(ks):
            column = pl.ds(pl.multiple_of((where[0] ^ k) * span, span), span)
            for i in range(count):
                refs[chips + i][:, column] = refs[n][i]

    out = jax.ShapeDtypeStruct((rows, chips * span), jnp.bfloat16)
    return call(kernel, [place], pieces, [out] * count)


def halves(where, rows):
    core = where[1]
    here = pl.ds(pl.multiple_of(core * rows, rows), rows)
    there = pl.ds(pl.multiple_of((1 - core) * rows, rows), rows)
    return here, there


def forward(place, partner, ks, pieces):
    chips = len(pieces)
    size = pieces[0].shape[1]

    def kernel(where, partner, *refs):
        keep, give, held, weights = refs[chips:]
        here, there = halves(where, size // 2)
        for n, k in enumerate(ks):
            held[where[0] ^ k, :3] = refs[n][...]
        for k in range(chips):
            b = where[0] ^ k
            p = partner[b]
            q = held[b, 0]
            s = mm(q, held[b, 1], NT) * SCALE
            t = mm(q, held[p, 1], NT) * SCALE
            peak = jnp.max(jnp.maximum(s, t), axis=1, keepdims=True)
            s, t = jnp.exp(s - peak), jnp.exp(t - peak)
            inverse = 1.0 / jnp.sum(s + t, axis=1, keepdims=True)
            s, t = s * inverse, t * inverse
            weights[b, 0] = s
            weights[b, 1] = t
            attended = mm(s.astype(jnp.bfloat16), held[b, 2], NN)
            attended += mm(t.astype(jnp.bfloat16), held[p, 2], NN)
            held[b, 3] = attended.astype(jnp.bfloat16)
            keep[k, 0] = held[b, 3, here]
            give[k, 0] = held[b, 3, there]

    half = jax.ShapeDtypeStruct((chips, 1, size // 2, HEAD), jnp.bfloat16)
    out_shape = [
        half,
        half,
        jax.ShapeDtypeStruct((chips, 4, size, HEAD), jnp.bfloat16),
        jax.ShapeDtypeStruct((chips, 2, size, size), jnp.float32),
    ]
    flops = chips * 8 * size * size * HEAD
    return call(kernel, [place, partner], pieces, out_shape, (), flops, chips * 2 * size * size)


def backward(place, partner, ks, pieces, held, weights):
    chips = len(pieces)
    size = held.shape[2]

    def kernel(where, partner, *refs):
        held, weights, keep, give, grads, acc_k, acc_v, grad_q = refs[chips:]
        here, there = halves(where, size // 2)
        for n, k in enumerate(ks):
            grads[where[0] ^ k] = refs[n][0]
        acc_k[...] = jnp.zeros_like(acc_k)
        acc_v[...] = jnp.zeros_like(acc_v)
        for k in range(chips):
            b = where[0] ^ k
            q, do = held[b, 0], grads[b]
            delta = jnp.sum(
                do.astype(jnp.float32) * held[b, 3].astype(jnp.float32), axis=1, keepdims=True
            )
            total = None
            for side, c in enumerate((b, partner[b])):
                w = weights[b, side]
                g = (w * (mm(do, held[c, 2], NT) - delta)).astype(jnp.bfloat16)
                term = mm(g, held[c, 1], NN)
                total = term if side == 0 else total + term
                acc_k[c] += mm(g, q, TN)
                acc_v[c] += mm(w.astype(jnp.bfloat16), do, TN)
            grad_q[k] = (SCALE * total).astype(jnp.bfloat16)
            keep[k, 0] = grad_q[k, here]
            give[k, 0] = grad_q[k, there]
        for k in range(chips):
            b = where[0] ^ k
            keep[k, 1] = (SCALE * acc_k[b, here]).astype(jnp.bfloat16)
            give[k, 1] = (SCALE * acc_k[b, there]).astype(jnp.bfloat16)
            keep[k, 2] = acc_v[b, here].astype(jnp.bfloat16)
            give[k, 2] = acc_v[b, there].astype(jnp.bfloat16)

    half = jax.ShapeDtypeStruct((chips, 3, size // 2, HEAD), jnp.bfloat16)
    scratch = [
        pltpu.VMEM((chips, size, HEAD), jnp.bfloat16),
        pltpu.VMEM((chips, size, HEAD), jnp.float32),
        pltpu.VMEM((chips, size, HEAD), jnp.float32),
        pltpu.VMEM((chips, size, HEAD), jnp.bfloat16),
    ]
    flops = chips * 16 * size * size * HEAD
    return call(
        kernel, [place, partner], [*pieces, held, weights], [half, half], scratch, flops
    )


def after(array, *earlier):
    return lax.optimization_barrier((array, *earlier))[0]


def by_permutes(queries, keys, values, cotangent, partner):
    devices = lax.axis_size("ctx")
    chips = devices // 2
    me = lax.axis_index("ctx")
    place = jnp.stack([me // 2, me % 2]).astype(jnp.int32)

    def hop(piece, distance):
        return lax.ppermute(piece, "ctx", [(i, i ^ distance) for i in range(devices)])

    far = list(range(chips // 2, chips))
    near = list(range(1, chips // 2))
    ks = [0, 1, *far[:-1], *near[1:-1], far[-1], near[-1]]

    def to_chips(pieces, ks):
        return {k: hop(pieces[k], 2 * k) for k in ks}

    def in_order(arrived):
        return [arrived[k] for k in ks]

    ins = [queries, keys, values]
    one = pack(place, ins, [hop(a, 1) for a in ins], chips)
    two = pack(place, [cotangent], [hop(cotangent, 1)], chips)
    first = {0: one[0]} | to_chips(one, far + near)
    second = {0: two[0]} | to_chips(two, far + near)
    keep, give, held, weights = forward(place, partner, ks, in_order(first))
    three = pair(place, keep, hop(after(give, *(second[k] for k in far[:-1])), 1))
    third = {0: three[0]} | to_chips(three, far)
    second[0] = after(two[0], three[0])
    keep, give = backward(place, partner, ks, in_order(second), held, weights)
    third |= to_chips([after(p, keep) for p in three], near)
    four = pair(place, keep, hop(after(give, *(third[k] for k in far[:-1])), 1))
    fourth = {0: four[0]} | to_chips(four, far + near)
    outs = unpack(place, ks, in_order(third)) + unpack(place, ks, in_order(fourth))
    return tuple(outs)


def body(queries, keys, values, cotangent, partner):
    rows, width = queries.shape
    devices = lax.axis_size("ctx")
    blocks = partner.shape[0]
    in_pairs = devices == 2 * blocks and devices * HEAD == width
    if in_pairs and blocks & (blocks - 1) == 0:
        return by_permutes(queries, keys, values, cotangent, partner)
    return by_all_to_all(queries, keys, values, cotangent, partner)


def solution(mesh):
    split = P(("dp", "ctx"), None)
    return jax.shard_map(
        body,
        mesh=mesh,
        in_specs=(split, split, split, split, P("dp")),
        out_specs=(split, split, split, split),
        check_vma=False,
    )
```

```python
import functools

import jax
import jax.numpy as jnp
from jax import lax
from jax.experimental import pallas as pl
from jax.experimental.pallas import tpu as pltpu
from jax.sharding import PartitionSpec as P

HEAD = 128
SCALE = HEAD ** (-0.5)

NN = (((1,), (0,)), ((), ()))
NT = (((1,), (1,)), ((), ()))
TN = (((0,), (0,)), ((), ()))


def mm(a, b, dims):
    return lax.dot_general(a, b, dims, preferred_element_type=jnp.float32)


def attention_kernel(pieces, blocks, first, partner, local, far, out, grad_k, grad_v, acc_k, acc_v):
    per_block = pieces // blocks
    block_rows = per_block * local.shape[2]
    total_blocks = acc_k.shape[0]

    def rows(ref, piece, which):
        return ref[pl.ds(piece * per_block, per_block), which].reshape(block_rows, HEAD)

    acc_k[...] = jnp.zeros_like(acc_k)
    acc_v[...] = jnp.zeros_like(acc_v)

    def one(b, carry):
        own = first[0] + b
        p = partner[own]
        q = rows(local, b, 0)
        do = rows(local, b, 3)
        ks, vs = [rows(local, b, 1)], [rows(local, b, 2)]
        if far is None:
            ks.append(rows(local, p, 1))
            vs.append(rows(local, p, 2))
        else:
            ks.append(rows(far, p, 0))
            vs.append(rows(far, p, 1))
        scores = [mm(q, k, NT) * SCALE for k in ks]
        peak = jnp.max(jnp.maximum(scores[0], scores[1]), axis=1, keepdims=True)
        exps = [jnp.exp(s - peak) for s in scores]
        total = jnp.sum(exps[0] + exps[1], axis=1, keepdims=True)
        inverse = 1.0 / total
        weights = [e * inverse for e in exps]
        coarse = [w.astype(jnp.bfloat16) for w in weights]
        attended = (mm(coarse[0], vs[0], NN) + mm(coarse[1], vs[1], NN)).astype(jnp.bfloat16)
        delta = jnp.sum(
            do.astype(jnp.float32) * attended.astype(jnp.float32), axis=1, keepdims=True
        )
        gs = [
            (w * (mm(do, v, NT) - delta)).astype(jnp.bfloat16) for w, v in zip(weights, vs)
        ]
        grad_q = (SCALE * (mm(gs[0], ks[0], NN) + mm(gs[1], ks[1], NN))).astype(jnp.bfloat16)
        here = pl.ds(b * per_block, per_block)
        out[here, 0] = attended.reshape(per_block, -1, HEAD)
        out[here, 1] = grad_q.reshape(per_block, -1, HEAD)
        for target, g, c in zip((own, p), gs, coarse):
            acc_k[target] += SCALE * mm(g, q, TN)
            acc_v[target] += mm(c, do, TN)
        return carry

    lax.fori_loop(0, blocks, one, 0)
    if grad_k is None:
        for which, acc in ((2, acc_k), (3, acc_v)):
            out[:, which] = acc[...].reshape(pieces, -1, HEAD).astype(jnp.bfloat16)
    else:
        grad_k[...] = acc_k[...]
        grad_v[...] = acc_v[...]


def attention(partner, first, local, far, blocks):
    pieces, _, rows, _ = local.shape
    total_blocks = partner.shape[0]
    block_rows = pieces // blocks * rows
    whole = far is None
    smem = pl.BlockSpec(memory_space=pltpu.SMEM)
    vmem = pl.BlockSpec(memory_space=pltpu.VMEM)
    grads = jax.ShapeDtypeStruct((total_blocks, block_rows, HEAD), jnp.float32)
    out_shape = [jax.ShapeDtypeStruct((pieces, 4 if whole else 2, rows, HEAD), jnp.bfloat16)]
    operands = [first, partner, local]
    if not whole:
        out_shape += [grads, grads]
        operands.append(far)

    def kernel(*refs):
        n = len(operands)
        m = n + len(out_shape)
        ins, outs, scratch = refs[:n], refs[n:m], refs[m:]
        attention_kernel(
            pieces,
            blocks,
            ins[0],
            ins[1],
            ins[2],
            None if whole else ins[3],
            outs[0],
            None if whole else outs[1],
            None if whole else outs[2],
            *scratch,
        )

    flops = 12 * blocks * block_rows * 2 * block_rows * HEAD
    return pl.pallas_call(
        kernel,
        out_shape=out_shape,
        in_specs=[smem, smem] + [vmem] * (len(operands) - 2),
        out_specs=[vmem] * len(out_shape),
        scratch_shapes=[pltpu.VMEM((total_blocks, block_rows, HEAD), jnp.float32)] * 2,
        compiler_params=pltpu.CompilerParams(vmem_limit_bytes=48 * 1024 * 1024),
        cost_estimate=pl.CostEstimate(
            flops=flops,
            bytes_accessed=2 * local.size * 2,
            transcendentals=blocks * block_rows * 2 * block_rows,
        ),
    )(*operands)


def by_all_to_all(queries, keys, values, cotangent, partner):
    rows, width = queries.shape
    devices = lax.axis_size("ctx")
    heads = width // HEAD
    blocks = partner.shape[0]
    spread = min(heads, devices)
    groups = devices // spread
    heads_here = heads // spread
    near = [[g * spread + i for i in range(spread)] for g in range(groups)]
    across = [[g * spread + i for g in range(groups)] for i in range(spread)]
    group = lax.axis_index("ctx") // spread
    exchange = functools.partial(
        lax.all_to_all,
        axis_name="ctx",
        split_axis=0,
        concat_axis=0,
        tiled=True,
        axis_index_groups=near if groups > 1 else None,
    )

    def pack(arrays):
        stacked = jnp.stack(arrays).reshape(len(arrays), rows, spread, heads_here, HEAD)
        return stacked.transpose(2, 3, 0, 1, 4)

    def unpack(packed):
        kinds = packed.shape[2]
        full = packed.transpose(2, 3, 0, 1, 4).reshape(kinds, rows, width)
        return [full[i] for i in range(kinds)]

    local_blocks = blocks // groups
    first = (group * local_blocks).astype(jnp.int32).reshape(1)
    local = exchange(pack([queries, keys, values, cotangent]))
    outs = []
    for h in range(heads_here):
        mine = local[:, h]
        if groups == 1:
            outs.append(attention(partner, first, mine, None, local_blocks)[0])
        else:
            far = lax.all_gather(
                mine[:, 1:3], "ctx", axis=0, tiled=True, axis_index_groups=across
            )
            out, grad_k, grad_v = attention(partner, first, mine, far, local_blocks)
            grads = lax.psum_scatter(
                jnp.stack([grad_k, grad_v], axis=1),
                "ctx",
                scatter_dimension=0,
                tiled=True,
                axis_index_groups=across,
            ).astype(jnp.bfloat16)
            grads = grads.transpose(0, 2, 1, 3).reshape(spread, rows, 2, HEAD).transpose(0, 2, 1, 3)
            outs.append(jnp.concatenate([out, grads], axis=1))
    return tuple(unpack(exchange(jnp.stack(outs, axis=1))))


def call(kernel, place, arrays, out_shape, scratch=(), flops=0, exps=0):
    smem = pl.BlockSpec(memory_space=pltpu.SMEM)
    vmem = pl.BlockSpec(memory_space=pltpu.VMEM)
    moved = sum(a.size * a.dtype.itemsize for a in arrays)
    moved += sum(a.size * a.dtype.itemsize for a in out_shape)
    return pl.pallas_call(
        kernel,
        out_shape=out_shape,
        in_specs=[smem] * len(place) + [vmem] * len(arrays),

        out_specs=[vmem] * len(out_shape),
        scratch_shapes=list(scratch),
        compiler_params=pltpu.CompilerParams(vmem_limit_bytes=40 * 1024 * 1024),
        cost_estimate=pl.CostEstimate(flops=flops, bytes_accessed=moved, transcendentals=exps),
    )(*place, *arrays)


def own_columns(place, arrays, chips):
    count = len(arrays)
    rows = arrays[0].shape[0]

    def kernel(where, *refs):
        for k in range(chips):
            column = pl.ds(pl.multiple_of(((where[0] ^ k) * 2 + where[1]) * HEAD, HEAD), HEAD)
            for i in range(count):
                refs[count][k, i] = refs[i][:, column]

    out = jax.ShapeDtypeStruct((chips, count, rows, HEAD), jnp.bfloat16)
    return call(kernel, [place], arrays, [out])[0]


def pack(place, ks, keeps, theirs):
    rows = keeps[0].shape[2]
    count = len(theirs)

    def kernel(where, *refs):
        here, there = halves(where, rows)
        keep = [(ref, i) for ref in refs[: len(keeps)] for i in range(ref.shape[1])]
        theirs = refs[len(keeps) : len(keeps) + count]
        for n, k in enumerate(ks):
            column = pl.ds(pl.multiple_of(((where[0] ^ k) * 2 + where[1]) * HEAD, HEAD), HEAD)
            out = refs[len(keeps) + count + n]
            for i, (ref, j) in enumerate(keep):
                out[i, here] = ref[k, j]
                out[i, there] = theirs[i][:, column]

    piece = jax.ShapeDtypeStruct((count, 2 * rows, HEAD), jnp.bfloat16)
    pieces = call(kernel, [place], [*keeps, *theirs], [piece] * len(ks))
    return dict(zip(ks, pieces))


def cut(place, pieces, bases, count):
    number = len(pieces)
    size = pieces[0].shape[1]

    def kernel(where, *refs):
        there = halves(where, size // 2)[1]
        for n in range(number):
            refs[number][n] = refs[n][bases[n] : bases[n] + count, there]

    out = jax.ShapeDtypeStruct((number, count, size // 2, HEAD), jnp.bfloat16)
    return call(kernel, [place], pieces, [out])[0]


def unpack(place, ks, pieces, bases, count, batches):
    chips = len(pieces)
    size = pieces[0].shape[1]

    def kernel(where, *refs):
        core = where[1]
        half = halves(where, size // 2)[0]
        outs = refs[chips + len(batches) :]
        got = [ref.at[n] for ref in refs[chips : chips + len(batches)] for n in range(ref.shape[0])]
        for n, k in enumerate(ks):
            start = (where[0] ^ k) * 2
            here = pl.ds(pl.multiple_of((start + core) * HEAD, HEAD), HEAD)
            there = pl.ds(pl.multiple_of((start + 1 - core) * HEAD, HEAD), HEAD)
            for i in range(count):
                outs[i][:, here] = refs[n][bases[n] + i, half]
                outs[i][:, there] = got[n][i]

    out = jax.ShapeDtypeStruct((size // 2, chips * 2 * HEAD), jnp.bfloat16)
    return call(kernel, [place], [*pieces, *batches], [out] * count)


def halves(where, rows):
    core = where[1]
    here = pl.ds(pl.multiple_of(core * rows, rows), rows)
    there = pl.ds(pl.multiple_of((1 - core) * rows, rows), rows)
    return here, there


def forward(place, partner, ks, far, pieces):
    chips = len(pieces)
    size = pieces[0].shape[1]

    def kernel(where, partner, *refs):
        outs = refs[chips:-2]
        held, weights = refs[-2:]
        for n, k in enumerate(ks):
            b = where[0] ^ k
            held[b, :3] = refs[n][:3]
            if k not in far:
                held[b, 4] = refs[n][3]
        for k in range(chips):
            b = where[0] ^ k
            p = partner[b]
            q = held[b, 0]
            s = mm(q, held[b, 1], NT) * SCALE
            t = mm(q, held[p, 1], NT) * SCALE
            peak = jnp.max(jnp.maximum(s, t), axis=1, keepdims=True)
            s, t = jnp.exp(s - peak), jnp.exp(t - peak)
            inverse = 1.0 / jnp.sum(s + t, axis=1, keepdims=True)
            s, t = s * inverse, t * inverse
            weights[b, 0] = s
            weights[b, 1] = t
            attended = mm(s.astype(jnp.bfloat16), held[b, 2], NN)
            attended += mm(t.astype(jnp.bfloat16), held[p, 2], NN)
            attended = attended.astype(jnp.bfloat16)
            held[b, 3] = attended
            if k in far:
                outs[far.index(k)][0] = attended

    out_shape = [
        *[jax.ShapeDtypeStruct((1, size, HEAD), jnp.bfloat16)] * len(far),
        jax.ShapeDtypeStruct((chips, 5, size, HEAD), jnp.bfloat16),
        jax.ShapeDtypeStruct((chips, 2, size, size), jnp.float32),
    ]
    flops = chips * 8 * size * size * HEAD
    outs = call(kernel, [place, partner], pieces, out_shape, (), flops, chips * 2 * size * size)
    return dict(zip(far, outs)), outs[-2], outs[-1]


def backward(place, partner, far, pieces, held, weights):
    chips, _, size, _ = held.shape

    def kernel(where, partner, *refs):
        ins = refs[: len(far)]
        held, weights = refs[len(far) : len(far) + 2]
        outs = refs[len(far) + 2 : len(far) + 2 + chips]
        acc_k, acc_v = refs[len(far) + 2 + chips :]
        acc_k[...] = jnp.zeros_like(acc_k)
        acc_v[...] = jnp.zeros_like(acc_v)
        for k in range(chips):
            b = where[0] ^ k
            q = held[b, 0]
            do = ins[far.index(k)][0] if k in far else held[b, 4]
            delta = jnp.sum(
                do.astype(jnp.float32) * held[b, 3].astype(jnp.float32), axis=1, keepdims=True
            )
            total = None
            for side, c in enumerate((b, partner[b])):
                w = weights[b, side]
                g = (w * (mm(do, held[c, 2], NT) - delta)).astype(jnp.bfloat16)
                term = mm(g, held[c, 1], NN)
                total = term if side == 0 else total + term
                acc_k[c] += mm(g, q, TN)
                acc_v[c] += mm(w.astype(jnp.bfloat16), do, TN)
            outs[k][0] = (SCALE * total).astype(jnp.bfloat16)
        for k in range(chips):
            b = where[0] ^ k
            outs[k][1] = (SCALE * acc_k[b]).astype(jnp.bfloat16)
            outs[k][2] = acc_v[b].astype(jnp.bfloat16)
            if k not in far:
                outs[k][3] = held[b, 3]

    out_shape = [
        jax.ShapeDtypeStruct((3 if k in far else 4, size, HEAD), jnp.bfloat16) for k in range(chips)
    ]
    scratch = [pltpu.VMEM((chips, size, HEAD), jnp.float32)] * 2
    flops = chips * 16 * size * size * HEAD
    outs = call(
        kernel, [place, partner], [*pieces, held, weights], out_shape, scratch, flops
    )
    return dict(enumerate(outs))


def after(array, *earlier):
    return lax.optimization_barrier((array, *earlier))[0]


def by_permutes(queries, keys, values, cotangent, partner):
    devices = lax.axis_size("ctx")
    chips = devices // 2
    me = lax.axis_index("ctx")
    place = jnp.stack([me // 2, me % 2]).astype(jnp.int32)

    def hop(piece, distance):
        return lax.ppermute(piece, "ctx", [(i, i ^ distance) for i in range(devices)])

    far = list(range(chips // 2, chips))
    near = list(range(1, chips // 2))
    ks = [0, *near[:1], *far[:2], *near[1:2], *far[2:3], *near[2:], *far[3:]]

    def to_chips(pieces, ks):
        return {k: hop(pieces[k], 2 * k) for k in ks}

    def in_order(arrived):
        return [arrived[k] for k in ks]

    ins = [queries, keys, values]
    theirs = [hop(a, 1) for a in ins]
    keep = own_columns(place, ins, chips)
    one = pack(place, far, [keep], theirs)
    their_do = hop(cotangent, 1)
    keep_do = own_columns(place, [cotangent], chips)
    one |= pack(place, [0, *near], [keep, keep_do], [*theirs, their_do])
    two = pack(place, far, [keep_do], [their_do])
    first = {0: one[0]} | to_chips(one, far + near)
    second = to_chips(two, far)
    three, held, weights = forward(place, partner, ks, far, in_order(first))
    third = {k: hop(after(three[k], second[k]), 2 * k) for k in far}
    four = backward(place, partner, far, [second[k] for k in far], held, weights)
    done = [third[k] for k in far]
    fourth = {0: four[0]} | {k: hop(after(four[k], *done), 2 * k) for k in far + near}
    third |= {k: fourth[k] for k in [0, *near]}
    bases = [0 if k in far else 3 for k in ks]
    third = in_order(third)
    third[0] = after(third[0], *(fourth[k] for k in far[:3]))
    outs = unpack(place, ks, third, bases, 1, [hop(cut(place, third, bases, 1), 1)])
    fourth = in_order(fourth)
    bases = [0] * chips
    batches = [hop(cut(place, fourth, bases, 3), 1)]
    return tuple(outs) + tuple(unpack(place, ks, fourth, bases, 3, batches))


def body(queries, keys, values, cotangent, partner):
    rows, width = queries.shape
    devices = lax.axis_size("ctx")
    blocks = partner.shape[0]
    in_pairs = devices == 2 * blocks and devices * HEAD == width
    if in_pairs and blocks & (blocks - 1) == 0:
        return by_permutes(queries, keys, values, cotangent, partner)
    return by_all_to_all(queries, keys, values, cotangent, partner)


def solution(mesh):
    split = P(("dp", "ctx"), None)
    return jax.shard_map(
        body,
        mesh=mesh,
        in_specs=(split, split, split, split, P("dp")),
        out_specs=(split, split, split, split),
        check_vma=False,
    )
```

```python
import functools

import jax
import jax.numpy as jnp
from jax import lax
from jax.experimental import pallas as pl
from jax.experimental.pallas import tpu as pltpu
from jax.sharding import PartitionSpec as P

HEAD = 128
SCALE = HEAD ** (-0.5)

NN = (((1,), (0,)), ((), ()))
NT = (((1,), (1,)), ((), ()))
TN = (((0,), (0,)), ((), ()))


def mm(a, b, dims):
    return lax.dot_general(a, b, dims, preferred_element_type=jnp.float32)


def attention_kernel(pieces, blocks, first, partner, local, far, out, grad_k, grad_v, acc_k, acc_v):
    per_block = pieces // blocks
    block_rows = per_block * local.shape[2]
    total_blocks = acc_k.shape[0]

    def rows(ref, piece, which):
        return ref[pl.ds(piece * per_block, per_block), which].reshape(block_rows, HEAD)

    acc_k[...] = jnp.zeros_like(acc_k)
    acc_v[...] = jnp.zeros_like(acc_v)

    def one(b, carry):
        own = first[0] + b
        p = partner[own]
        q = rows(local, b, 0)
        do = rows(local, b, 3)
        ks, vs = [rows(local, b, 1)], [rows(local, b, 2)]
        if far is None:
            ks.append(rows(local, p, 1))
            vs.append(rows(local, p, 2))
        else:
            ks.append(rows(far, p, 0))
            vs.append(rows(far, p, 1))
        scores = [mm(q, k, NT) * SCALE for k in ks]
        peak = jnp.max(jnp.maximum(scores[0], scores[1]), axis=1, keepdims=True)
        exps = [jnp.exp(s - peak) for s in scores]
        total = jnp.sum(exps[0] + exps[1], axis=1, keepdims=True)
        inverse = 1.0 / total
        weights = [e * inverse for e in exps]
        coarse = [w.astype(jnp.bfloat16) for w in weights]
        attended = (mm(coarse[0], vs[0], NN) + mm(coarse[1], vs[1], NN)).astype(jnp.bfloat16)
        delta = jnp.sum(
            do.astype(jnp.float32) * attended.astype(jnp.float32), axis=1, keepdims=True
        )
        gs = [
            (w * (mm(do, v, NT) - delta)).astype(jnp.bfloat16) for w, v in zip(weights, vs)
        ]
        grad_q = (SCALE * (mm(gs[0], ks[0], NN) + mm(gs[1], ks[1], NN))).astype(jnp.bfloat16)
        here = pl.ds(b * per_block, per_block)
        out[here, 0] = attended.reshape(per_block, -1, HEAD)
        out[here, 1] = grad_q.reshape(per_block, -1, HEAD)
        for target, g, c in zip((own, p), gs, coarse):
            acc_k[target] += SCALE * mm(g, q, TN)
            acc_v[target] += mm(c, do, TN)
        return carry

    lax.fori_loop(0, blocks, one, 0)
    if grad_k is None:
        for which, acc in ((2, acc_k), (3, acc_v)):
            out[:, which] = acc[...].reshape(pieces, -1, HEAD).astype(jnp.bfloat16)
    else:
        grad_k[...] = acc_k[...]
        grad_v[...] = acc_v[...]


def attention(partner, first, local, far, blocks):
    pieces, _, rows, _ = local.shape
    total_blocks = partner.shape[0]
    block_rows = pieces // blocks * rows
    whole = far is None
    smem = pl.BlockSpec(memory_space=pltpu.SMEM)
    vmem = pl.BlockSpec(memory_space=pltpu.VMEM)
    grads = jax.ShapeDtypeStruct((total_blocks, block_rows, HEAD), jnp.float32)
    out_shape = [jax.ShapeDtypeStruct((pieces, 4 if whole else 2, rows, HEAD), jnp.bfloat16)]
    operands = [first, partner, local]
    if not whole:
        out_shape += [grads, grads]
        operands.append(far)

    def kernel(*refs):
        n = len(operands)
        m = n + len(out_shape)
        ins, outs, scratch = refs[:n], refs[n:m], refs[m:]
        attention_kernel(
            pieces,
            blocks,
            ins[0],
            ins[1],
            ins[2],
            None if whole else ins[3],
            outs[0],
            None if whole else outs[1],
            None if whole else outs[2],
            *scratch,
        )

    flops = 12 * blocks * block_rows * 2 * block_rows * HEAD
    return pl.pallas_call(
        kernel,
        out_shape=out_shape,
        in_specs=[smem, smem] + [vmem] * (len(operands) - 2),
        out_specs=[vmem] * len(out_shape),
        scratch_shapes=[pltpu.VMEM((total_blocks, block_rows, HEAD), jnp.float32)] * 2,
        compiler_params=pltpu.CompilerParams(vmem_limit_bytes=48 * 1024 * 1024),
        cost_estimate=pl.CostEstimate(
            flops=flops,
            bytes_accessed=2 * local.size * 2,
            transcendentals=blocks * block_rows * 2 * block_rows,
        ),
    )(*operands)


def by_all_to_all(queries, keys, values, cotangent, partner):
    rows, width = queries.shape
    devices = lax.axis_size("ctx")
    heads = width // HEAD
    blocks = partner.shape[0]
    spread = min(heads, devices)
    groups = devices // spread
    heads_here = heads // spread
    near = [[g * spread + i for i in range(spread)] for g in range(groups)]
    across = [[g * spread + i for g in range(groups)] for i in range(spread)]
    group = lax.axis_index("ctx") // spread
    exchange = functools.partial(
        lax.all_to_all,
        axis_name="ctx",
        split_axis=0,
        concat_axis=0,
        tiled=True,
        axis_index_groups=near if groups > 1 else None,
    )

    def pack(arrays):
        stacked = jnp.stack(arrays).reshape(len(arrays), rows, spread, heads_here, HEAD)
        return stacked.transpose(2, 3, 0, 1, 4)

    def unpack(packed):
        kinds = packed.shape[2]
        full = packed.transpose(2, 3, 0, 1, 4).reshape(kinds, rows, width)
        return [full[i] for i in range(kinds)]

    local_blocks = blocks // groups
    first = (group * local_blocks).astype(jnp.int32).reshape(1)
    local = exchange(pack([queries, keys, values, cotangent]))
    outs = []
    for h in range(heads_here):
        mine = local[:, h]
        if groups == 1:
            outs.append(attention(partner, first, mine, None, local_blocks)[0])
        else:
            far = lax.all_gather(
                mine[:, 1:3], "ctx", axis=0, tiled=True, axis_index_groups=across
            )
            out, grad_k, grad_v = attention(partner, first, mine, far, local_blocks)
            grads = lax.psum_scatter(
                jnp.stack([grad_k, grad_v], axis=1),
                "ctx",
                scatter_dimension=0,
                tiled=True,
                axis_index_groups=across,
            ).astype(jnp.bfloat16)
            grads = grads.transpose(0, 2, 1, 3).reshape(spread, rows, 2, HEAD).transpose(0, 2, 1, 3)
            outs.append(jnp.concatenate([out, grads], axis=1))
    return tuple(unpack(exchange(jnp.stack(outs, axis=1))))


def call(kernel, place, arrays, out_shape, scratch=(), flops=0, exps=0):
    smem = pl.BlockSpec(memory_space=pltpu.SMEM)
    vmem = pl.BlockSpec(memory_space=pltpu.VMEM)
    moved = sum(a.size * a.dtype.itemsize for a in arrays)
    moved += sum(a.size * a.dtype.itemsize for a in out_shape)
    return pl.pallas_call(
        kernel,
        out_shape=out_shape,
        in_specs=[smem] * len(place) + [vmem] * len(arrays),

        out_specs=[vmem] * len(out_shape),
        scratch_shapes=list(scratch),
        compiler_params=pltpu.CompilerParams(vmem_limit_bytes=40 * 1024 * 1024),
        cost_estimate=pl.CostEstimate(flops=flops, bytes_accessed=moved, transcendentals=exps),
    )(*place, *arrays)


def own_columns(place, arrays, chips):
    count = len(arrays)
    rows = arrays[0].shape[0]

    def kernel(where, *refs):
        out, sems = refs[count:]
        copies = []
        for k in range(chips):
            column = pl.ds(pl.multiple_of(((where[0] ^ k) * 2 + where[1]) * HEAD, HEAD), HEAD)
            for i in range(count):
                copies.append(
                    pltpu.make_async_copy(refs[i].at[:, column], out.at[k, i], sems.at[k, i])
                )
        for copy in copies:
            copy.start()
        for copy in copies:
            copy.wait()

    return pl.pallas_call(
        kernel,
        out_shape=jax.ShapeDtypeStruct((chips, count, rows, HEAD), jnp.bfloat16),
        in_specs=[pl.BlockSpec(memory_space=pltpu.SMEM)] + [pl.BlockSpec(memory_space=pltpu.HBM)] * count,
        out_specs=pl.BlockSpec(memory_space=pltpu.VMEM),
        scratch_shapes=[pltpu.SemaphoreType.DMA((chips, count))],
        compiler_params=pltpu.CompilerParams(vmem_limit_bytes=40 * 1024 * 1024),
    )(place, *[pltpu.with_memory_space_constraint(a, pltpu.HBM) for a in arrays])


def pack(place, ks, keeps, theirs):
    rows = keeps[0].shape[2]
    count = len(theirs)

    def kernel(where, *refs):
        here, there = halves(where, rows)
        keep = [(ref, i) for ref in refs[: len(keeps)] for i in range(ref.shape[1])]
        theirs = refs[len(keeps) : len(keeps) + count]
        for n, k in enumerate(ks):
            column = pl.ds(pl.multiple_of(((where[0] ^ k) * 2 + where[1]) * HEAD, HEAD), HEAD)
            out = refs[len(keeps) + count + n]
            for i, (ref, j) in enumerate(keep):
                out[i, here] = ref[k, j]
                out[i, there] = theirs[i][:, column]

    piece = jax.ShapeDtypeStruct((count, 2 * rows, HEAD), jnp.bfloat16)
    pieces = call(kernel, [place], [*keeps, *theirs], [piece] * len(ks))
    return dict(zip(ks, pieces))


def cut(place, pieces, bases, count):
    number = len(pieces)
    size = pieces[0].shape[1]

    def kernel(where, *refs):
        there = halves(where, size // 2)[1]
        for n in range(number):
            refs[number][n] = refs[n][bases[n] : bases[n] + count, there]

    out = jax.ShapeDtypeStruct((number, count, size // 2, HEAD), jnp.bfloat16)
    return call(kernel, [place], pieces, [out])[0]


def unpack(place, ks, pieces, bases, count, batches):
    chips = len(pieces)
    size = pieces[0].shape[1]

    def kernel(where, *refs):
        core = where[1]
        half = halves(where, size // 2)[0]
        outs = refs[chips + len(batches) :]
        got = [ref.at[n] for ref in refs[chips : chips + len(batches)] for n in range(ref.shape[0])]
        for n, k in enumerate(ks):
            start = (where[0] ^ k) * 2
            here = pl.ds(pl.multiple_of((start + core) * HEAD, HEAD), HEAD)
            there = pl.ds(pl.multiple_of((start + 1 - core) * HEAD, HEAD), HEAD)
            for i in range(count):
                outs[i][:, here] = refs[n][bases[n] + i, half]
                outs[i][:, there] = got[n][i]

    out = jax.ShapeDtypeStruct((size // 2, chips * 2 * HEAD), jnp.bfloat16)
    return call(kernel, [place], [*pieces, *batches], [out] * count)


def halves(where, rows):
    core = where[1]
    here = pl.ds(pl.multiple_of(core * rows, rows), rows)
    there = pl.ds(pl.multiple_of((1 - core) * rows, rows), rows)
    return here, there


def forward(place, partner, ks, far, pieces):
    chips = len(pieces)
    size = pieces[0].shape[1]

    def kernel(where, partner, *refs):
        outs = refs[chips:-2]
        held, weights = refs[-2:]
        for n, k in enumerate(ks):
            b = where[0] ^ k
            held[b, :3] = refs[n][:3]
            if k not in far:
                held[b, 4] = refs[n][3]
        for k in range(chips):
            b = where[0] ^ k
            p = partner[b]
            q = held[b, 0]
            s = mm(q, held[b, 1], NT) * SCALE
            t = mm(q, held[p, 1], NT) * SCALE
            peak = jnp.max(jnp.maximum(s, t), axis=1, keepdims=True)
            s, t = jnp.exp(s - peak), jnp.exp(t - peak)
            inverse = 1.0 / jnp.sum(s + t, axis=1, keepdims=True)
            s, t = s * inverse, t * inverse
            weights[b, 0] = s
            weights[b, 1] = t
            attended = mm(s.astype(jnp.bfloat16), held[b, 2], NN)
            attended += mm(t.astype(jnp.bfloat16), held[p, 2], NN)
            attended = attended.astype(jnp.bfloat16)
            held[b, 3] = attended
            if k in far:
                outs[far.index(k)][0] = attended

    out_shape = [
        *[jax.ShapeDtypeStruct((1, size, HEAD), jnp.bfloat16)] * len(far),
        jax.ShapeDtypeStruct((chips, 5, size, HEAD), jnp.bfloat16),
        jax.ShapeDtypeStruct((chips, 2, size, size), jnp.float32),
    ]
    flops = chips * 8 * size * size * HEAD
    outs = call(kernel, [place, partner], pieces, out_shape, (), flops, chips * 2 * size * size)
    return dict(zip(far, outs)), outs[-2], outs[-1]


def backward(place, partner, far, pieces, held, weights):
    chips, _, size, _ = held.shape

    def kernel(where, partner, *refs):
        ins = refs[: len(far)]
        held, weights = refs[len(far) : len(far) + 2]
        outs = refs[len(far) + 2 : len(far) + 2 + chips]
        acc_k, acc_v = refs[len(far) + 2 + chips :]
        acc_k[...] = jnp.zeros_like(acc_k)
        acc_v[...] = jnp.zeros_like(acc_v)
        for k in range(chips):
            b = where[0] ^ k
            q = held[b, 0]
            do = ins[far.index(k)][0] if k in far else held[b, 4]
            delta = jnp.sum(
                do.astype(jnp.float32) * held[b, 3].astype(jnp.float32), axis=1, keepdims=True
            )
            total = None
            for side, c in enumerate((b, partner[b])):
                w = weights[b, side]
                g = (w * (mm(do, held[c, 2], NT) - delta)).astype(jnp.bfloat16)
                term = mm(g, held[c, 1], NN)
                total = term if side == 0 else total + term
                acc_k[c] += mm(g, q, TN)
                acc_v[c] += mm(w.astype(jnp.bfloat16), do, TN)
            outs[k][0] = (SCALE * total).astype(jnp.bfloat16)
        for k in range(chips):
            b = where[0] ^ k
            outs[k][1] = (SCALE * acc_k[b]).astype(jnp.bfloat16)
            outs[k][2] = acc_v[b].astype(jnp.bfloat16)
            if k not in far:
                outs[k][3] = held[b, 3]

    out_shape = [
        jax.ShapeDtypeStruct((3 if k in far else 4, size, HEAD), jnp.bfloat16) for k in range(chips)
    ]
    scratch = [pltpu.VMEM((chips, size, HEAD), jnp.float32)] * 2
    flops = chips * 16 * size * size * HEAD
    outs = call(
        kernel, [place, partner], [*pieces, held, weights], out_shape, scratch, flops
    )
    return dict(enumerate(outs))


def after(array, *earlier):
    return lax.optimization_barrier((array, *earlier))[0]


def by_permutes(queries, keys, values, cotangent, partner):
    devices = lax.axis_size("ctx")
    chips = devices // 2
    me = lax.axis_index("ctx")
    place = jnp.stack([me // 2, me % 2]).astype(jnp.int32)

    def hop(piece, distance):
        return lax.ppermute(piece, "ctx", [(i, i ^ distance) for i in range(devices)])

    far = list(range(chips // 2, chips))
    near = list(range(1, chips // 2))
    ks = [0, *near[:1], *far[:2], *near[1:2], *far[2:3], *near[2:], *far[3:]]

    def to_chips(pieces, ks):
        return {k: hop(pieces[k], 2 * k) for k in ks}

    def in_order(arrived):
        return [arrived[k] for k in ks]

    ins = [queries, keys, values]
    theirs = [hop(a, 1) for a in ins]
    keep = own_columns(place, ins, chips)
    one = pack(place, far, [keep], theirs)
    their_do = hop(cotangent, 1)
    keep_do = own_columns(place, [cotangent], chips)
    one |= pack(place, [0, *near], [keep, keep_do], [*theirs, their_do])
    two = pack(place, far, [keep_do], [their_do])
    first = {0: one[0]} | to_chips(one, far + near)
    second = to_chips(two, far)
    three, held, weights = forward(place, partner, ks, far, in_order(first))
    third = {k: hop(after(three[k], second[k]), 2 * k) for k in far}
    four = backward(place, partner, far, [second[k] for k in far], held, weights)
    done = [third[k] for k in far]
    fourth = {0: four[0]} | {k: hop(after(four[k], *done), 2 * k) for k in far + near}
    third |= {k: fourth[k] for k in [0, *near]}
    bases = [0 if k in far else 3 for k in ks]
    third = in_order(third)
    third[0] = after(third[0], *(fourth[k] for k in far[:3]))
    outs = unpack(place, ks, third, bases, 1, [hop(cut(place, third, bases, 1), 1)])
    fourth = in_order(fourth)
    bases = [0] * chips
    batches = [hop(cut(place, fourth, bases, 3), 1)]
    return tuple(outs) + tuple(unpack(place, ks, fourth, bases, 3, batches))


def body(queries, keys, values, cotangent, partner):
    rows, width = queries.shape
    devices = lax.axis_size("ctx")
    blocks = partner.shape[0]
    in_pairs = devices == 2 * blocks and devices * HEAD == width
    if in_pairs and blocks & (blocks - 1) == 0:
        return by_permutes(queries, keys, values, cotangent, partner)
    return by_all_to_all(queries, keys, values, cotangent, partner)


def solution(mesh):
    split = P(("dp", "ctx"), None)
    return jax.shard_map(
        body,
        mesh=mesh,
        in_specs=(split, split, split, split, P("dp")),
        out_specs=(split, split, split, split),
        check_vma=False,
    )
```

```python
import functools

import jax
import jax.numpy as jnp
from jax import lax
from jax.experimental import pallas as pl
from jax.experimental.pallas import tpu as pltpu
from jax.sharding import PartitionSpec as P

HEAD = 128
SCALE = HEAD ** (-0.5)

NN = (((1,), (0,)), ((), ()))
NT = (((1,), (1,)), ((), ()))
TN = (((0,), (0,)), ((), ()))


def mm(a, b, dims):
    return lax.dot_general(a, b, dims, preferred_element_type=jnp.float32)


def attention_kernel(pieces, blocks, first, partner, local, far, out, grad_k, grad_v, acc_k, acc_v):
    per_block = pieces // blocks
    block_rows = per_block * local.shape[2]
    total_blocks = acc_k.shape[0]

    def rows(ref, piece, which):
        return ref[pl.ds(piece * per_block, per_block), which].reshape(block_rows, HEAD)

    acc_k[...] = jnp.zeros_like(acc_k)
    acc_v[...] = jnp.zeros_like(acc_v)

    def one(b, carry):
        own = first[0] + b
        p = partner[own]
        q = rows(local, b, 0)
        do = rows(local, b, 3)
        ks, vs = [rows(local, b, 1)], [rows(local, b, 2)]
        if far is None:
            ks.append(rows(local, p, 1))
            vs.append(rows(local, p, 2))
        else:
            ks.append(rows(far, p, 0))
            vs.append(rows(far, p, 1))
        scores = [mm(q, k, NT) * SCALE for k in ks]
        peak = jnp.max(jnp.maximum(scores[0], scores[1]), axis=1, keepdims=True)
        exps = [jnp.exp(s - peak) for s in scores]
        total = jnp.sum(exps[0] + exps[1], axis=1, keepdims=True)
        inverse = 1.0 / total
        weights = [e * inverse for e in exps]
        coarse = [w.astype(jnp.bfloat16) for w in weights]
        attended = (mm(coarse[0], vs[0], NN) + mm(coarse[1], vs[1], NN)).astype(jnp.bfloat16)
        delta = jnp.sum(
            do.astype(jnp.float32) * attended.astype(jnp.float32), axis=1, keepdims=True
        )
        gs = [
            (w * (mm(do, v, NT) - delta)).astype(jnp.bfloat16) for w, v in zip(weights, vs)
        ]
        grad_q = (SCALE * (mm(gs[0], ks[0], NN) + mm(gs[1], ks[1], NN))).astype(jnp.bfloat16)
        here = pl.ds(b * per_block, per_block)
        out[here, 0] = attended.reshape(per_block, -1, HEAD)
        out[here, 1] = grad_q.reshape(per_block, -1, HEAD)
        for target, g, c in zip((own, p), gs, coarse):
            acc_k[target] += SCALE * mm(g, q, TN)
            acc_v[target] += mm(c, do, TN)
        return carry

    lax.fori_loop(0, blocks, one, 0)
    if grad_k is None:
        for which, acc in ((2, acc_k), (3, acc_v)):
            out[:, which] = acc[...].reshape(pieces, -1, HEAD).astype(jnp.bfloat16)
    else:
        grad_k[...] = acc_k[...]
        grad_v[...] = acc_v[...]


def attention(partner, first, local, far, blocks):
    pieces, _, rows, _ = local.shape
    total_blocks = partner.shape[0]
    block_rows = pieces // blocks * rows
    whole = far is None
    smem = pl.BlockSpec(memory_space=pltpu.SMEM)
    vmem = pl.BlockSpec(memory_space=pltpu.VMEM)
    grads = jax.ShapeDtypeStruct((total_blocks, block_rows, HEAD), jnp.float32)
    out_shape = [jax.ShapeDtypeStruct((pieces, 4 if whole else 2, rows, HEAD), jnp.bfloat16)]
    operands = [first, partner, local]
    if not whole:
        out_shape += [grads, grads]
        operands.append(far)

    def kernel(*refs):
        n = len(operands)
        m = n + len(out_shape)
        ins, outs, scratch = refs[:n], refs[n:m], refs[m:]
        attention_kernel(
            pieces,
            blocks,
            ins[0],
            ins[1],
            ins[2],
            None if whole else ins[3],
            outs[0],
            None if whole else outs[1],
            None if whole else outs[2],
            *scratch,
        )

    flops = 12 * blocks * block_rows * 2 * block_rows * HEAD
    return pl.pallas_call(
        kernel,
        out_shape=out_shape,
        in_specs=[smem, smem] + [vmem] * (len(operands) - 2),
        out_specs=[vmem] * len(out_shape),
        scratch_shapes=[pltpu.VMEM((total_blocks, block_rows, HEAD), jnp.float32)] * 2,
        compiler_params=pltpu.CompilerParams(vmem_limit_bytes=48 * 1024 * 1024),
        cost_estimate=pl.CostEstimate(
            flops=flops,
            bytes_accessed=2 * local.size * 2,
            transcendentals=blocks * block_rows * 2 * block_rows,
        ),
    )(*operands)


def by_all_to_all(queries, keys, values, cotangent, partner):
    rows, width = queries.shape
    devices = lax.axis_size("ctx")
    heads = width // HEAD
    blocks = partner.shape[0]
    spread = min(heads, devices)
    groups = devices // spread
    heads_here = heads // spread
    near = [[g * spread + i for i in range(spread)] for g in range(groups)]
    across = [[g * spread + i for g in range(groups)] for i in range(spread)]
    group = lax.axis_index("ctx") // spread
    exchange = functools.partial(
        lax.all_to_all,
        axis_name="ctx",
        split_axis=0,
        concat_axis=0,
        tiled=True,
        axis_index_groups=near if groups > 1 else None,
    )

    def pack(arrays):
        stacked = jnp.stack(arrays).reshape(len(arrays), rows, spread, heads_here, HEAD)
        return stacked.transpose(2, 3, 0, 1, 4)

    def unpack(packed):
        kinds = packed.shape[2]
        full = packed.transpose(2, 3, 0, 1, 4).reshape(kinds, rows, width)
        return [full[i] for i in range(kinds)]

    local_blocks = blocks // groups
    first = (group * local_blocks).astype(jnp.int32).reshape(1)
    local = exchange(pack([queries, keys, values, cotangent]))
    outs = []
    for h in range(heads_here):
        mine = local[:, h]
        if groups == 1:
            outs.append(attention(partner, first, mine, None, local_blocks)[0])
        else:
            far = lax.all_gather(
                mine[:, 1:3], "ctx", axis=0, tiled=True, axis_index_groups=across
            )
            out, grad_k, grad_v = attention(partner, first, mine, far, local_blocks)
            grads = lax.psum_scatter(
                jnp.stack([grad_k, grad_v], axis=1),
                "ctx",
                scatter_dimension=0,
                tiled=True,
                axis_index_groups=across,
            ).astype(jnp.bfloat16)
            grads = grads.transpose(0, 2, 1, 3).reshape(spread, rows, 2, HEAD).transpose(0, 2, 1, 3)
            outs.append(jnp.concatenate([out, grads], axis=1))
    return tuple(unpack(exchange(jnp.stack(outs, axis=1))))


def call(kernel, place, arrays, out_shape, scratch=(), flops=0, exps=0):
    smem = pl.BlockSpec(memory_space=pltpu.SMEM)
    vmem = pl.BlockSpec(memory_space=pltpu.VMEM)
    moved = sum(a.size * a.dtype.itemsize for a in arrays)
    moved += sum(a.size * a.dtype.itemsize for a in out_shape)
    return pl.pallas_call(
        kernel,
        out_shape=out_shape,
        in_specs=[smem] * len(place) + [vmem] * len(arrays),

        out_specs=[vmem] * len(out_shape),
        scratch_shapes=list(scratch),
        compiler_params=pltpu.CompilerParams(vmem_limit_bytes=40 * 1024 * 1024),
        cost_estimate=pl.CostEstimate(flops=flops, bytes_accessed=moved, transcendentals=exps),
    )(*place, *arrays)


def own_columns(place, arrays, chips):
    count = len(arrays)
    rows = arrays[0].shape[0]

    def kernel(where, *refs):
        out, sems = refs[count:]
        copies = []
        for k in range(chips):
            column = pl.ds(pl.multiple_of(((where[0] ^ k) * 2 + where[1]) * HEAD, HEAD), HEAD)
            for i in range(count):
                copies.append(
                    pltpu.make_async_copy(refs[i].at[:, column], out.at[k, i], sems.at[k, i])
                )
        for copy in copies:
            copy.start()
        for copy in copies:
            copy.wait()

    return pl.pallas_call(
        kernel,
        out_shape=jax.ShapeDtypeStruct((chips, count, rows, HEAD), jnp.bfloat16),
        in_specs=[pl.BlockSpec(memory_space=pltpu.SMEM)] + [pl.BlockSpec(memory_space=pltpu.HBM)] * count,
        out_specs=pl.BlockSpec(memory_space=pltpu.VMEM),
        scratch_shapes=[pltpu.SemaphoreType.DMA((chips, count))],
        compiler_params=pltpu.CompilerParams(vmem_limit_bytes=40 * 1024 * 1024),
    )(place, *[pltpu.with_memory_space_constraint(a, pltpu.HBM) for a in arrays])


def own_rows(place, k, arrays):
    count = len(arrays)
    rows = arrays[0].shape[0]
    span = 2 * HEAD

    def kernel(where, *refs):
        out, sems = refs[count:]
        column = pl.ds(pl.multiple_of((where[0] ^ k) * span, span), span)
        copies = [
            pltpu.make_async_copy(refs[i].at[:, column], out.at[i], sems.at[i])
            for i in range(count)
        ]
        for copy in copies:
            copy.start()
        for copy in copies:
            copy.wait()

    return pl.pallas_call(
        kernel,
        out_shape=jax.ShapeDtypeStruct((count, rows, span), jnp.bfloat16),
        in_specs=[pl.BlockSpec(memory_space=pltpu.SMEM)]
        + [pl.BlockSpec(memory_space=pltpu.HBM)] * count,
        out_specs=pl.BlockSpec(memory_space=pltpu.VMEM),
        scratch_shapes=[pltpu.SemaphoreType.DMA((count,))],
        compiler_params=pltpu.CompilerParams(vmem_limit_bytes=40 * 1024 * 1024),
    )(place, *[pltpu.with_memory_space_constraint(a, pltpu.HBM) for a in arrays])


def other_head(place, piece):
    count, rows, _ = piece.shape

    def kernel(where, piece, out):
        out[...] = piece[:, :, pl.ds(pl.multiple_of((1 - where[1]) * HEAD, HEAD), HEAD)]

    out = jax.ShapeDtypeStruct((count, rows, HEAD), jnp.bfloat16)
    return call(kernel, [place], [piece], [out])[0]


def pack(place, ks, keeps, theirs):
    rows = keeps[0].shape[2]
    count = len(theirs)

    def kernel(where, *refs):
        here, there = halves(where, rows)
        keep = [(ref, i) for ref in refs[: len(keeps)] for i in range(ref.shape[1])]
        theirs = refs[len(keeps) : len(keeps) + count]
        for n, k in enumerate(ks):
            column = pl.ds(pl.multiple_of(((where[0] ^ k) * 2 + where[1]) * HEAD, HEAD), HEAD)
            out = refs[len(keeps) + count + n]
            for i, (ref, j) in enumerate(keep):
                out[i, here] = ref[k, j]
                out[i, there] = theirs[i][:, column]

    piece = jax.ShapeDtypeStruct((count, 2 * rows, HEAD), jnp.bfloat16)
    pieces = call(kernel, [place], [*keeps, *theirs], [piece] * len(ks))
    return dict(zip(ks, pieces))


def cut(place, pieces, bases, count):
    number = len(pieces)
    size = pieces[0].shape[1]

    def kernel(where, *refs):
        there = halves(where, size // 2)[1]
        for n in range(number):
            refs[number][n] = refs[n][bases[n] : bases[n] + count, there]

    out = jax.ShapeDtypeStruct((number, count, size // 2, HEAD), jnp.bfloat16)
    return call(kernel, [place], pieces, [out])[0]


def unpack_once(place, ks, pieces, bases, got):
    chips = len(pieces)
    size = pieces[0].shape[1]

    def kernel(where, *refs):
        core = where[1]
        half = halves(where, size // 2)[0]
        for n, k in enumerate(ks):
            start = (where[0] ^ k) * 2
            here = pl.ds(pl.multiple_of((start + core) * HEAD, HEAD), HEAD)
            there = pl.ds(pl.multiple_of((start + 1 - core) * HEAD, HEAD), HEAD)
            refs[chips + 1][:, here] = refs[n][bases[n], half]
            refs[chips + 1][:, there] = refs[chips][n, 0]

    out = jax.ShapeDtypeStruct((size // 2, chips * 2 * HEAD), jnp.bfloat16)
    return call(kernel, [place], [*pieces, got], [out])


def scatter(place, ks, arrays, picks, other, results, width):
    count = len(picks)
    rows = arrays[0].shape[-2] if other else arrays[0].shape[-2] // 2
    total = len(ks) * count

    def kernel(where, *refs):
        core = where[1]
        half = halves(where, rows)[0]
        outs, sems = refs[-1 - count : -1], refs[-1]
        copies = []
        for n, k in enumerate(ks):
            head = (where[0] ^ k) * 2 + (1 - core if other else core)
            column = pl.ds(pl.multiple_of(head * HEAD, HEAD), HEAD)
            for i in range(count):
                array, index = picks[i][n]
                source = refs[array].at[index] if other else refs[array].at[index, half]
                copies.append(
                    pltpu.make_async_copy(source, outs[i].at[:, column], sems.at[n * count + i])
                )
        for copy in copies:
            copy.start()
        for copy in copies:
            copy.wait()

    smem = pl.BlockSpec(memory_space=pltpu.SMEM)
    vmem = pl.BlockSpec(memory_space=pltpu.VMEM)
    hbm = pl.BlockSpec(memory_space=pltpu.HBM)
    out = jax.ShapeDtypeStruct((rows, width), jnp.bfloat16)
    moved = 2 * count * len(ks) * rows * HEAD * 2
    return pl.pallas_call(
        kernel,
        out_shape=[out] * count,
        in_specs=[smem] + [vmem] * len(arrays) + [hbm] * len(results),
        out_specs=[hbm] * count,
        scratch_shapes=[pltpu.SemaphoreType.DMA((total,))],
        input_output_aliases={1 + len(arrays) + i: i for i in range(len(results))},
        compiler_params=pltpu.CompilerParams(vmem_limit_bytes=40 * 1024 * 1024),
        cost_estimate=pl.CostEstimate(flops=0, bytes_accessed=moved, transcendentals=0),
    )(place, *arrays, *results)


def unpack(place, ks, pieces, bases, count, got):
    width = len(ks) * 2 * HEAD
    picks = [[(n, bases[n] + i) for n in range(len(ks))] for i in range(count)]
    outs = scatter(place, ks, pieces, picks, False, [], width)
    picks = [[(0, (n, i)) for n in range(len(ks))] for i in range(count)]
    return scatter(place, ks, [got], picks, True, outs, width)


def halves(where, rows):
    core = where[1]
    here = pl.ds(pl.multiple_of(core * rows, rows), rows)
    there = pl.ds(pl.multiple_of((1 - core) * rows, rows), rows)
    return here, there


def forward(place, partner, ks, far, early, pieces):
    chips = len(pieces) + 1
    size = pieces[0].shape[1]

    def kernel(where, partner, mine, theirs, *refs):
        outs = refs[len(pieces) : -2]
        held, weights = refs[-2:]
        here, there = halves(where, size // 2)
        column = pl.ds(pl.multiple_of(where[1] * HEAD, HEAD), HEAD)
        for i in range(3):
            held[where[0] ^ far[0], i, here] = mine[i, :, column]
            held[where[0] ^ far[0], i, there] = theirs[i]
        for n, k in enumerate(ks):
            b = where[0] ^ k
            held[b, :3] = refs[n][:3]
            if k not in far:
                held[b, 4] = refs[n][3]
        for k in range(chips):
            b = where[0] ^ k
            p = partner[b]
            q = held[b, 0]
            s = mm(q, held[b, 1], NT) * SCALE
            t = mm(q, held[p, 1], NT) * SCALE
            peak = jnp.max(jnp.maximum(s, t), axis=1, keepdims=True)
            s, t = jnp.exp(s - peak), jnp.exp(t - peak)
            inverse = 1.0 / jnp.sum(s + t, axis=1, keepdims=True)
            s, t = s * inverse, t * inverse
            weights[b, 0] = s
            weights[b, 1] = t
            attended = mm(s.astype(jnp.bfloat16), held[b, 2], NN)
            attended += mm(t.astype(jnp.bfloat16), held[p, 2], NN)
            attended = attended.astype(jnp.bfloat16)
            held[b, 3] = attended
            if k in far:
                outs[far.index(k)][0] = attended

    out_shape = [
        *[jax.ShapeDtypeStruct((1, size, HEAD), jnp.bfloat16)] * len(far),
        jax.ShapeDtypeStruct((chips, 5, size, HEAD), jnp.bfloat16),
        jax.ShapeDtypeStruct((chips, 2, size, size), jnp.float32),
    ]
    flops = chips * 8 * size * size * HEAD
    exps = chips * 2 * size * size
    outs = call(kernel, [place, partner], [*early, *pieces], out_shape, (), flops, exps)
    return dict(zip(far, outs)), outs[-2], outs[-1]


def backward(place, partner, far, pieces, held, weights):
    chips, _, size, _ = held.shape

    def kernel(where, partner, *refs):
        ins = refs[: len(far)]
        held, weights = refs[len(far) : len(far) + 2]
        outs = refs[len(far) + 2 : len(far) + 2 + chips]
        acc_k, acc_v = refs[len(far) + 2 + chips :]
        acc_k[...] = jnp.zeros_like(acc_k)
        acc_v[...] = jnp.zeros_like(acc_v)
        for k in range(chips):
            b = where[0] ^ k
            q = held[b, 0]
            do = ins[far.index(k)][0] if k in far else held[b, 4]
            delta = jnp.sum(
                do.astype(jnp.float32) * held[b, 3].astype(jnp.float32), axis=1, keepdims=True
            )
            total = None
            for side, c in enumerate((b, partner[b])):
                w = weights[b, side]
                g = (w * (mm(do, held[c, 2], NT) - delta)).astype(jnp.bfloat16)
                term = mm(g, held[c, 1], NN)
                total = term if side == 0 else total + term
                acc_k[c] += mm(g, q, TN)
                acc_v[c] += mm(w.astype(jnp.bfloat16), do, TN)
            outs[k][0] = (SCALE * total).astype(jnp.bfloat16)
        for k in range(chips):
            b = where[0] ^ k
            outs[k][1] = (SCALE * acc_k[b]).astype(jnp.bfloat16)
            outs[k][2] = acc_v[b].astype(jnp.bfloat16)
            if k not in far:
                outs[k][3] = held[b, 3]

    out_shape = [
        jax.ShapeDtypeStruct((3 if k in far else 4, size, HEAD), jnp.bfloat16) for k in range(chips)
    ]
    scratch = [pltpu.VMEM((chips, size, HEAD), jnp.float32)] * 2
    flops = chips * 16 * size * size * HEAD
    outs = call(
        kernel, [place, partner], [*pieces, held, weights], out_shape, scratch, flops
    )
    return dict(enumerate(outs))


def after(array, *earlier):
    return lax.optimization_barrier((array, *earlier))[0]


def by_permutes(queries, keys, values, cotangent, partner):
    devices = lax.axis_size("ctx")
    chips = devices // 2
    me = lax.axis_index("ctx")
    place = jnp.stack([me // 2, me % 2]).astype(jnp.int32)

    def hop(piece, distance):
        return lax.ppermute(piece, "ctx", [(i, i ^ distance) for i in range(devices)])

    far = list(range(chips // 2, chips))
    near = list(range(1, chips // 2))
    ks = [0, *near[:1], *far[:2], *near[1:2], *far[2:3], *near[2:], *far[3:]]

    def to_chips(pieces, ks):
        return {k: hop(pieces[k], 2 * k) for k in ks}

    def in_order(arrived):
        return [arrived[k] for k in ks]

    ins = [queries, keys, values]
    theirs = [hop(a, 1) for a in ins]
    early = own_rows(place, far[0], ins)
    keep = own_columns(after(place, early), ins, chips)
    one = pack(place, far[1:], [keep], theirs)
    their_do = hop(cotangent, 1)
    keep_do = own_columns(place, [cotangent], chips)
    one |= pack(place, [0, *near], [keep, keep_do], [*theirs, their_do])
    two = pack(place, far, [keep_do], [their_do])
    first = {0: one[0]} | to_chips(one, far[1:] + near)
    second = to_chips(two, far)
    early = hop(early, 2 * far[0])
    early = [early, hop(other_head(after(place, first[far[2]]), early), 1)]
    later = [k for k in ks if k != far[0]]
    first = [first[k] for k in later]
    three, held, weights = forward(place, partner, later, far, early, first)
    third = {k: hop(after(three[k], second[k]), 2 * k) for k in far}
    four = backward(place, partner, far, [second[k] for k in far], held, weights)
    done = [third[k] for k in far]
    fourth = {0: four[0]} | {k: hop(after(four[k], *done), 2 * k) for k in far + near}
    third |= {k: fourth[k] for k in [0, *near]}
    bases = [0 if k in far else 3 for k in ks]
    third = in_order(third)
    third[0] = after(third[0], *(fourth[k] for k in far[:3]))
    outs = unpack_once(place, ks, third, bases, hop(cut(place, third, bases, 1), 1))
    fourth = in_order(fourth)
    bases = [0] * chips
    got = hop(cut(place, fourth, bases, 3), 1)
    return tuple(outs) + tuple(unpack(place, ks, fourth, bases, 3, got))


def body(queries, keys, values, cotangent, partner):
    rows, width = queries.shape
    devices = lax.axis_size("ctx")
    blocks = partner.shape[0]
    in_pairs = devices == 2 * blocks and devices * HEAD == width
    if in_pairs and blocks & (blocks - 1) == 0:
        return by_permutes(queries, keys, values, cotangent, partner)
    return by_all_to_all(queries, keys, values, cotangent, partner)


def solution(mesh):
    split = P(("dp", "ctx"), None)
    return jax.shard_map(
        body,
        mesh=mesh,
        in_specs=(split, split, split, split, P("dp")),
        out_specs=(split, split, split, split),
        check_vma=False,
    )
```

```python
import functools

import jax
import jax.numpy as jnp
from jax import lax
from jax.experimental import pallas as pl
from jax.experimental.pallas import tpu as pltpu
from jax.sharding import PartitionSpec as P

HEAD = 128
SCALE = HEAD ** (-0.5)

NN = (((1,), (0,)), ((), ()))
NT = (((1,), (1,)), ((), ()))
TN = (((0,), (0,)), ((), ()))


def mm(a, b, dims):
    return lax.dot_general(a, b, dims, preferred_element_type=jnp.float32)


def attention_kernel(pieces, blocks, first, partner, local, far, out, grad_k, grad_v, acc_k, acc_v):
    per_block = pieces // blocks
    block_rows = per_block * local.shape[2]
    total_blocks = acc_k.shape[0]

    def rows(ref, piece, which):
        return ref[pl.ds(piece * per_block, per_block), which].reshape(block_rows, HEAD)

    acc_k[...] = jnp.zeros_like(acc_k)
    acc_v[...] = jnp.zeros_like(acc_v)

    def one(b, carry):
        own = first[0] + b
        p = partner[own]
        q = rows(local, b, 0)
        do = rows(local, b, 3)
        ks, vs = [rows(local, b, 1)], [rows(local, b, 2)]
        if far is None:
            ks.append(rows(local, p, 1))
            vs.append(rows(local, p, 2))
        else:
            ks.append(rows(far, p, 0))
            vs.append(rows(far, p, 1))
        scores = [mm(q, k, NT) * SCALE for k in ks]
        peak = jnp.max(jnp.maximum(scores[0], scores[1]), axis=1, keepdims=True)
        exps = [jnp.exp(s - peak) for s in scores]
        total = jnp.sum(exps[0] + exps[1], axis=1, keepdims=True)
        inverse = 1.0 / total
        weights = [e * inverse for e in exps]
        coarse = [w.astype(jnp.bfloat16) for w in weights]
        attended = (mm(coarse[0], vs[0], NN) + mm(coarse[1], vs[1], NN)).astype(jnp.bfloat16)
        delta = jnp.sum(
            do.astype(jnp.float32) * attended.astype(jnp.float32), axis=1, keepdims=True
        )
        gs = [
            (w * (mm(do, v, NT) - delta)).astype(jnp.bfloat16) for w, v in zip(weights, vs)
        ]
        grad_q = (SCALE * (mm(gs[0], ks[0], NN) + mm(gs[1], ks[1], NN))).astype(jnp.bfloat16)
        here = pl.ds(b * per_block, per_block)
        out[here, 0] = attended.reshape(per_block, -1, HEAD)
        out[here, 1] = grad_q.reshape(per_block, -1, HEAD)
        for target, g, c in zip((own, p), gs, coarse):
            acc_k[target] += SCALE * mm(g, q, TN)
            acc_v[target] += mm(c, do, TN)
        return carry

    lax.fori_loop(0, blocks, one, 0)
    if grad_k is None:
        for which, acc in ((2, acc_k), (3, acc_v)):
            out[:, which] = acc[...].reshape(pieces, -1, HEAD).astype(jnp.bfloat16)
    else:
        grad_k[...] = acc_k[...]
        grad_v[...] = acc_v[...]


def attention(partner, first, local, far, blocks):
    pieces, _, rows, _ = local.shape
    total_blocks = partner.shape[0]
    block_rows = pieces // blocks * rows
    whole = far is None
    smem = pl.BlockSpec(memory_space=pltpu.SMEM)
    vmem = pl.BlockSpec(memory_space=pltpu.VMEM)
    grads = jax.ShapeDtypeStruct((total_blocks, block_rows, HEAD), jnp.float32)
    out_shape = [jax.ShapeDtypeStruct((pieces, 4 if whole else 2, rows, HEAD), jnp.bfloat16)]
    operands = [first, partner, local]
    if not whole:
        out_shape += [grads, grads]
        operands.append(far)

    def kernel(*refs):
        n = len(operands)
        m = n + len(out_shape)
        ins, outs, scratch = refs[:n], refs[n:m], refs[m:]
        attention_kernel(
            pieces,
            blocks,
            ins[0],
            ins[1],
            ins[2],
            None if whole else ins[3],
            outs[0],
            None if whole else outs[1],
            None if whole else outs[2],
            *scratch,
        )

    flops = 12 * blocks * block_rows * 2 * block_rows * HEAD
    return pl.pallas_call(
        kernel,
        out_shape=out_shape,
        in_specs=[smem, smem] + [vmem] * (len(operands) - 2),
        out_specs=[vmem] * len(out_shape),
        scratch_shapes=[pltpu.VMEM((total_blocks, block_rows, HEAD), jnp.float32)] * 2,
        compiler_params=pltpu.CompilerParams(vmem_limit_bytes=48 * 1024 * 1024),
        cost_estimate=pl.CostEstimate(
            flops=flops,
            bytes_accessed=2 * local.size * 2,
            transcendentals=blocks * block_rows * 2 * block_rows,
        ),
    )(*operands)


def by_all_to_all(queries, keys, values, cotangent, partner):
    rows, width = queries.shape
    devices = lax.axis_size("ctx")
    heads = width // HEAD
    blocks = partner.shape[0]
    spread = min(heads, devices)
    groups = devices // spread
    heads_here = heads // spread
    near = [[g * spread + i for i in range(spread)] for g in range(groups)]
    across = [[g * spread + i for g in range(groups)] for i in range(spread)]
    group = lax.axis_index("ctx") // spread
    exchange = functools.partial(
        lax.all_to_all,
        axis_name="ctx",
        split_axis=0,
        concat_axis=0,
        tiled=True,
        axis_index_groups=near if groups > 1 else None,
    )

    def pack(arrays):
        stacked = jnp.stack(arrays).reshape(len(arrays), rows, spread, heads_here, HEAD)
        return stacked.transpose(2, 3, 0, 1, 4)

    def unpack(packed):
        kinds = packed.shape[2]
        full = packed.transpose(2, 3, 0, 1, 4).reshape(kinds, rows, width)
        return [full[i] for i in range(kinds)]

    local_blocks = blocks // groups
    first = (group * local_blocks).astype(jnp.int32).reshape(1)
    local = exchange(pack([queries, keys, values, cotangent]))
    outs = []
    for h in range(heads_here):
        mine = local[:, h]
        if groups == 1:
            outs.append(attention(partner, first, mine, None, local_blocks)[0])
        else:
            far = lax.all_gather(
                mine[:, 1:3], "ctx", axis=0, tiled=True, axis_index_groups=across
            )
            out, grad_k, grad_v = attention(partner, first, mine, far, local_blocks)
            grads = lax.psum_scatter(
                jnp.stack([grad_k, grad_v], axis=1),
                "ctx",
                scatter_dimension=0,
                tiled=True,
                axis_index_groups=across,
            ).astype(jnp.bfloat16)
            grads = grads.transpose(0, 2, 1, 3).reshape(spread, rows, 2, HEAD).transpose(0, 2, 1, 3)
            outs.append(jnp.concatenate([out, grads], axis=1))
    return tuple(unpack(exchange(jnp.stack(outs, axis=1))))


def call(kernel, place, arrays, out_shape, scratch=(), flops=0, exps=0):
    smem = pl.BlockSpec(memory_space=pltpu.SMEM)
    vmem = pl.BlockSpec(memory_space=pltpu.VMEM)
    moved = sum(a.size * a.dtype.itemsize for a in arrays)
    moved += sum(a.size * a.dtype.itemsize for a in out_shape)
    return pl.pallas_call(
        kernel,
        out_shape=out_shape,
        in_specs=[smem] * len(place) + [vmem] * len(arrays),

        out_specs=[vmem] * len(out_shape),
        scratch_shapes=list(scratch),
        compiler_params=pltpu.CompilerParams(vmem_limit_bytes=40 * 1024 * 1024),
        cost_estimate=pl.CostEstimate(flops=flops, bytes_accessed=moved, transcendentals=exps),
    )(*place, *arrays)


def own_columns(place, arrays, chips):
    count = len(arrays)
    rows = arrays[0].shape[0]

    def kernel(where, *refs):
        out, sems = refs[count:]
        copies = []
        for k in range(chips):
            column = pl.ds(pl.multiple_of(((where[0] ^ k) * 2 + where[1]) * HEAD, HEAD), HEAD)
            for i in range(count):
                copies.append(
                    pltpu.make_async_copy(refs[i].at[:, column], out.at[k, i], sems.at[k, i])
                )
        for copy in copies:
            copy.start()
        for copy in copies:
            copy.wait()

    return pl.pallas_call(
        kernel,
        out_shape=jax.ShapeDtypeStruct((chips, count, rows, HEAD), jnp.bfloat16),
        in_specs=[pl.BlockSpec(memory_space=pltpu.SMEM)] + [pl.BlockSpec(memory_space=pltpu.HBM)] * count,
        out_specs=pl.BlockSpec(memory_space=pltpu.VMEM),
        scratch_shapes=[pltpu.SemaphoreType.DMA((chips, count))],
        compiler_params=pltpu.CompilerParams(vmem_limit_bytes=40 * 1024 * 1024),
    )(place, *[pltpu.with_memory_space_constraint(a, pltpu.HBM) for a in arrays])


def own_rows(place, k, arrays):
    count = len(arrays)
    rows = arrays[0].shape[0]
    span = 2 * HEAD

    def kernel(where, *refs):
        out, sems = refs[count:]
        column = pl.ds(pl.multiple_of((where[0] ^ k) * span, span), span)
        copies = [
            pltpu.make_async_copy(refs[i].at[:, column], out.at[i], sems.at[i])
            for i in range(count)
        ]
        for copy in copies:
            copy.start()
        for copy in copies:
            copy.wait()

    return pl.pallas_call(
        kernel,
        out_shape=jax.ShapeDtypeStruct((count, rows, span), jnp.bfloat16),
        in_specs=[pl.BlockSpec(memory_space=pltpu.SMEM)]
        + [pl.BlockSpec(memory_space=pltpu.HBM)] * count,
        out_specs=pl.BlockSpec(memory_space=pltpu.VMEM),
        scratch_shapes=[pltpu.SemaphoreType.DMA((count,))],
        compiler_params=pltpu.CompilerParams(vmem_limit_bytes=40 * 1024 * 1024),
    )(place, *[pltpu.with_memory_space_constraint(a, pltpu.HBM) for a in arrays])


def other_head(place, piece):
    count, rows, _ = piece.shape

    def kernel(where, piece, out):
        out[...] = piece[:, :, pl.ds(pl.multiple_of((1 - where[1]) * HEAD, HEAD), HEAD)]

    out = jax.ShapeDtypeStruct((count, rows, HEAD), jnp.bfloat16)
    return call(kernel, [place], [piece], [out])[0]


def pack(place, ks, keeps, theirs):
    rows = keeps[0].shape[2]
    count = len(theirs)

    def kernel(where, *refs):
        here, there = halves(where, rows)
        keep = [(ref, i) for ref in refs[: len(keeps)] for i in range(ref.shape[1])]
        theirs = refs[len(keeps) : len(keeps) + count]
        for n, k in enumerate(ks):
            column = pl.ds(pl.multiple_of(((where[0] ^ k) * 2 + where[1]) * HEAD, HEAD), HEAD)
            out = refs[len(keeps) + count + n]
            for i, (ref, j) in enumerate(keep):
                out[i, here] = ref[k, j]
                out[i, there] = theirs[i][:, column]

    piece = jax.ShapeDtypeStruct((count, 2 * rows, HEAD), jnp.bfloat16)
    pieces = call(kernel, [place], [*keeps, *theirs], [piece] * len(ks))
    return dict(zip(ks, pieces))


def cut(place, pieces, bases, count):
    number = len(pieces)
    size = pieces[0].shape[1]

    def kernel(where, *refs):
        there = halves(where, size // 2)[1]
        for n in range(number):
            refs[number][n] = refs[n][bases[n] : bases[n] + count, there]

    out = jax.ShapeDtypeStruct((number, count, size // 2, HEAD), jnp.bfloat16)
    return call(kernel, [place], pieces, [out])[0]


def scatter(place, ks, arrays, picks, other, results, width):
    count = len(picks)
    rows = arrays[0].shape[-2] if other else arrays[0].shape[-2] // 2
    total = len(ks) * count

    def kernel(where, *refs):
        core = where[1]
        half = halves(where, rows)[0]
        outs, sems = refs[-1 - count : -1], refs[-1]
        copies = []
        for n, k in enumerate(ks):
            head = (where[0] ^ k) * 2 + (1 - core if other else core)
            column = pl.ds(pl.multiple_of(head * HEAD, HEAD), HEAD)
            for i in range(count):
                array, index = picks[i][n]
                source = refs[array].at[index] if other else refs[array].at[index, half]
                copies.append(
                    pltpu.make_async_copy(source, outs[i].at[:, column], sems.at[n * count + i])
                )
        for copy in copies:
            copy.start()
        for copy in copies:
            copy.wait()

    smem = pl.BlockSpec(memory_space=pltpu.SMEM)
    vmem = pl.BlockSpec(memory_space=pltpu.VMEM)
    hbm = pl.BlockSpec(memory_space=pltpu.HBM)
    out = jax.ShapeDtypeStruct((rows, width), jnp.bfloat16)
    moved = 2 * count * len(ks) * rows * HEAD * 2
    return pl.pallas_call(
        kernel,
        out_shape=[out] * count,
        in_specs=[smem] + [vmem] * len(arrays) + [hbm] * len(results),
        out_specs=[hbm] * count,
        scratch_shapes=[pltpu.SemaphoreType.DMA((total,))],
        input_output_aliases={1 + len(arrays) + i: i for i in range(len(results))},
        compiler_params=pltpu.CompilerParams(vmem_limit_bytes=40 * 1024 * 1024),
        cost_estimate=pl.CostEstimate(flops=0, bytes_accessed=moved, transcendentals=0),
    )(place, *arrays, *results)


def unpack(place, ks, third, fourth, bases, got_attended, got_grads):
    width = len(ks) * 2 * HEAD
    chips = range(len(ks))
    picks = [[(n, bases[n]) for n in chips]]
    picks += [[(len(ks) + n, i) for n in chips] for i in range(3)]
    outs = scatter(place, ks, [*third, *fourth], picks, False, [], width)
    picks = [[(0, (n, 0)) for n in chips]]
    picks += [[(1, (n, i)) for n in chips] for i in range(3)]
    return scatter(place, ks, [got_attended, got_grads], picks, True, outs, width)


def halves(where, rows):
    core = where[1]
    here = pl.ds(pl.multiple_of(core * rows, rows), rows)
    there = pl.ds(pl.multiple_of((1 - core) * rows, rows), rows)
    return here, there


def forward(place, partner, ks, far, early, pieces):
    chips = len(pieces) + 1
    size = pieces[0].shape[1]

    def kernel(where, partner, mine, theirs, *refs):
        outs = refs[len(pieces) : -2]
        held, weights = refs[-2:]
        here, there = halves(where, size // 2)
        column = pl.ds(pl.multiple_of(where[1] * HEAD, HEAD), HEAD)
        for i in range(3):
            held[where[0] ^ far[0], i, here] = mine[i, :, column]
            held[where[0] ^ far[0], i, there] = theirs[i]
        for n, k in enumerate(ks):
            b = where[0] ^ k
            held[b, :3] = refs[n][:3]
            if k not in far:
                held[b, 4] = refs[n][3]
        for k in range(chips):
            b = where[0] ^ k
            p = partner[b]
            q = held[b, 0]
            s = mm(q, held[b, 1], NT) * SCALE
            t = mm(q, held[p, 1], NT) * SCALE
            peak = jnp.max(jnp.maximum(s, t), axis=1, keepdims=True)
            s, t = jnp.exp(s - peak), jnp.exp(t - peak)
            inverse = 1.0 / jnp.sum(s + t, axis=1, keepdims=True)
            s, t = s * inverse, t * inverse
            weights[b, 0] = s
            weights[b, 1] = t
            attended = mm(s.astype(jnp.bfloat16), held[b, 2], NN)
            attended += mm(t.astype(jnp.bfloat16), held[p, 2], NN)
            attended = attended.astype(jnp.bfloat16)
            held[b, 3] = attended
            if k in far:
                outs[far.index(k)][0] = attended

    out_shape = [
        *[jax.ShapeDtypeStruct((1, size, HEAD), jnp.bfloat16)] * len(far),
        jax.ShapeDtypeStruct((chips, 5, size, HEAD), jnp.bfloat16),
        jax.ShapeDtypeStruct((chips, 2, size, size), jnp.float32),
    ]
    flops = chips * 8 * size * size * HEAD
    exps = chips * 2 * size * size
    outs = call(kernel, [place, partner], [*early, *pieces], out_shape, (), flops, exps)
    return dict(zip(far, outs)), outs[-2], outs[-1]


def backward(place, partner, far, pieces, held, weights):
    chips, _, size, _ = held.shape

    def kernel(where, partner, *refs):
        ins = refs[: len(far)]
        held, weights = refs[len(far) : len(far) + 2]
        outs = refs[len(far) + 2 : len(far) + 2 + chips]
        acc_k, acc_v = refs[len(far) + 2 + chips :]
        acc_k[...] = jnp.zeros_like(acc_k)
        acc_v[...] = jnp.zeros_like(acc_v)
        for k in range(chips):
            b = where[0] ^ k
            q = held[b, 0]
            do = ins[far.index(k)][0] if k in far else held[b, 4]
            delta = jnp.sum(
                do.astype(jnp.float32) * held[b, 3].astype(jnp.float32), axis=1, keepdims=True
            )
            total = None
            for side, c in enumerate((b, partner[b])):
                w = weights[b, side]
                g = (w * (mm(do, held[c, 2], NT) - delta)).astype(jnp.bfloat16)
                term = mm(g, held[c, 1], NN)
                total = term if side == 0 else total + term
                acc_k[c] += mm(g, q, TN)
                acc_v[c] += mm(w.astype(jnp.bfloat16), do, TN)
            outs[k][0] = (SCALE * total).astype(jnp.bfloat16)
        for k in range(chips):
            b = where[0] ^ k
            outs[k][1] = (SCALE * acc_k[b]).astype(jnp.bfloat16)
            outs[k][2] = acc_v[b].astype(jnp.bfloat16)
            if k not in far:
                outs[k][3] = held[b, 3]

    out_shape = [
        jax.ShapeDtypeStruct((3 if k in far else 4, size, HEAD), jnp.bfloat16) for k in range(chips)
    ]
    scratch = [pltpu.VMEM((chips, size, HEAD), jnp.float32)] * 2
    flops = chips * 16 * size * size * HEAD
    outs = call(
        kernel, [place, partner], [*pieces, held, weights], out_shape, scratch, flops
    )
    return dict(enumerate(outs))


def after(array, *earlier):
    return lax.optimization_barrier((array, *earlier))[0]


def by_permutes(queries, keys, values, cotangent, partner):
    devices = lax.axis_size("ctx")
    chips = devices // 2
    me = lax.axis_index("ctx")
    place = jnp.stack([me // 2, me % 2]).astype(jnp.int32)

    def hop(piece, distance):
        return lax.ppermute(piece, "ctx", [(i, i ^ distance) for i in range(devices)])

    far = list(range(chips // 2, chips))
    near = list(range(1, chips // 2))
    ks = [0, *near[:1], *far[:2], *near[1:2], *far[2:3], *near[2:], *far[3:]]

    def to_chips(pieces, ks):
        return {k: hop(pieces[k], 2 * k) for k in ks}

    def in_order(arrived):
        return [arrived[k] for k in ks]

    ins = [queries, keys, values]
    theirs = [hop(a, 1) for a in ins]
    early = own_rows(place, far[0], ins)
    keep = own_columns(after(place, early), ins, chips)
    one = pack(place, far[1:], [keep], theirs)
    their_do = hop(cotangent, 1)
    keep_do = own_columns(place, [cotangent], chips)
    one |= pack(place, [0, *near], [keep, keep_do], [*theirs, their_do])
    two = pack(place, far, [keep_do], [their_do])
    first = {0: one[0]} | to_chips(one, far[1:] + near)
    second = to_chips(two, far)
    early = hop(early, 2 * far[0])
    early = [early, hop(other_head(after(place, first[far[2]]), early), 1)]
    later = [k for k in ks if k != far[0]]
    first = [first[k] for k in later]
    three, held, weights = forward(place, partner, later, far, early, first)
    third = {k: hop(after(three[k], second[k]), 2 * k) for k in far}
    four = backward(place, partner, far, [second[k] for k in far], held, weights)
    done = [third[k] for k in far]
    fourth = {0: four[0]} | {k: hop(after(four[k], *done), 2 * k) for k in far + near}
    third |= {k: fourth[k] for k in [0, *near]}
    bases = [0 if k in far else 3 for k in ks]
    third = in_order(third)
    third[0] = after(third[0], *(fourth[k] for k in far[:3]))
    got_attended = hop(cut(place, third, bases, 1), 1)
    fourth = in_order(fourth)
    got_grads = hop(cut(place, fourth, [0] * chips, 3), 1)
    return tuple(unpack(place, ks, third, fourth, bases, got_attended, got_grads))


def body(queries, keys, values, cotangent, partner):
    rows, width = queries.shape
    devices = lax.axis_size("ctx")
    blocks = partner.shape[0]
    in_pairs = devices == 2 * blocks and devices * HEAD == width
    if in_pairs and blocks & (blocks - 1) == 0:
        return by_permutes(queries, keys, values, cotangent, partner)
    return by_all_to_all(queries, keys, values, cotangent, partner)


def solution(mesh):
    split = P(("dp", "ctx"), None)
    return jax.shard_map(
        body,
        mesh=mesh,
        in_specs=(split, split, split, split, P("dp")),
        out_specs=(split, split, split, split),
        check_vma=False,
    )
```

```python
import functools

import jax
import jax.numpy as jnp
from jax import lax
from jax.experimental import pallas as pl
from jax.experimental.pallas import tpu as pltpu
from jax.sharding import PartitionSpec as P

HEAD = 128
SCALE = HEAD ** (-0.5)

NN = (((1,), (0,)), ((), ()))
NT = (((1,), (1,)), ((), ()))
TN = (((0,), (0,)), ((), ()))


def mm(a, b, dims):
    return lax.dot_general(a, b, dims, preferred_element_type=jnp.float32)


def attention_kernel(pieces, blocks, first, partner, local, far, out, grad_k, grad_v, acc_k, acc_v):
    per_block = pieces // blocks
    block_rows = per_block * local.shape[2]
    total_blocks = acc_k.shape[0]

    def rows(ref, piece, which):
        return ref[pl.ds(piece * per_block, per_block), which].reshape(block_rows, HEAD)

    acc_k[...] = jnp.zeros_like(acc_k)
    acc_v[...] = jnp.zeros_like(acc_v)

    def one(b, carry):
        own = first[0] + b
        p = partner[own]
        q = rows(local, b, 0)
        do = rows(local, b, 3)
        ks, vs = [rows(local, b, 1)], [rows(local, b, 2)]
        if far is None:
            ks.append(rows(local, p, 1))
            vs.append(rows(local, p, 2))
        else:
            ks.append(rows(far, p, 0))
            vs.append(rows(far, p, 1))
        scores = [mm(q, k, NT) * SCALE for k in ks]
        peak = jnp.max(jnp.maximum(scores[0], scores[1]), axis=1, keepdims=True)
        exps = [jnp.exp(s - peak) for s in scores]
        total = jnp.sum(exps[0] + exps[1], axis=1, keepdims=True)
        inverse = 1.0 / total
        weights = [e * inverse for e in exps]
        coarse = [w.astype(jnp.bfloat16) for w in weights]
        attended = (mm(coarse[0], vs[0], NN) + mm(coarse[1], vs[1], NN)).astype(jnp.bfloat16)
        delta = jnp.sum(
            do.astype(jnp.float32) * attended.astype(jnp.float32), axis=1, keepdims=True
        )
        gs = [
            (w * (mm(do, v, NT) - delta)).astype(jnp.bfloat16) for w, v in zip(weights, vs)
        ]
        grad_q = (SCALE * (mm(gs[0], ks[0], NN) + mm(gs[1], ks[1], NN))).astype(jnp.bfloat16)
        here = pl.ds(b * per_block, per_block)
        out[here, 0] = attended.reshape(per_block, -1, HEAD)
        out[here, 1] = grad_q.reshape(per_block, -1, HEAD)
        for target, g, c in zip((own, p), gs, coarse):
            acc_k[target] += SCALE * mm(g, q, TN)
            acc_v[target] += mm(c, do, TN)
        return carry

    lax.fori_loop(0, blocks, one, 0)
    if grad_k is None:
        for which, acc in ((2, acc_k), (3, acc_v)):
            out[:, which] = acc[...].reshape(pieces, -1, HEAD).astype(jnp.bfloat16)
    else:
        grad_k[...] = acc_k[...]
        grad_v[...] = acc_v[...]


def attention(partner, first, local, far, blocks):
    pieces, _, rows, _ = local.shape
    total_blocks = partner.shape[0]
    block_rows = pieces // blocks * rows
    whole = far is None
    smem = pl.BlockSpec(memory_space=pltpu.SMEM)
    vmem = pl.BlockSpec(memory_space=pltpu.VMEM)
    grads = jax.ShapeDtypeStruct((total_blocks, block_rows, HEAD), jnp.float32)
    out_shape = [jax.ShapeDtypeStruct((pieces, 4 if whole else 2, rows, HEAD), jnp.bfloat16)]
    operands = [first, partner, local]
    if not whole:
        out_shape += [grads, grads]
        operands.append(far)

    def kernel(*refs):
        n = len(operands)
        m = n + len(out_shape)
        ins, outs, scratch = refs[:n], refs[n:m], refs[m:]
        attention_kernel(
            pieces,
            blocks,
            ins[0],
            ins[1],
            ins[2],
            None if whole else ins[3],
            outs[0],
            None if whole else outs[1],
            None if whole else outs[2],
            *scratch,
        )

    flops = 12 * blocks * block_rows * 2 * block_rows * HEAD
    return pl.pallas_call(
        kernel,
        out_shape=out_shape,
        in_specs=[smem, smem] + [vmem] * (len(operands) - 2),
        out_specs=[vmem] * len(out_shape),
        scratch_shapes=[pltpu.VMEM((total_blocks, block_rows, HEAD), jnp.float32)] * 2,
        compiler_params=pltpu.CompilerParams(vmem_limit_bytes=48 * 1024 * 1024),
        cost_estimate=pl.CostEstimate(
            flops=flops,
            bytes_accessed=2 * local.size * 2,
            transcendentals=blocks * block_rows * 2 * block_rows,
        ),
    )(*operands)


def by_all_to_all(queries, keys, values, cotangent, partner):
    rows, width = queries.shape
    devices = lax.axis_size("ctx")
    heads = width // HEAD
    blocks = partner.shape[0]
    spread = min(heads, devices)
    groups = devices // spread
    heads_here = heads // spread
    near = [[g * spread + i for i in range(spread)] for g in range(groups)]
    across = [[g * spread + i for g in range(groups)] for i in range(spread)]
    group = lax.axis_index("ctx") // spread
    exchange = functools.partial(
        lax.all_to_all,
        axis_name="ctx",
        split_axis=0,
        concat_axis=0,
        tiled=True,
        axis_index_groups=near if groups > 1 else None,
    )

    def pack(arrays):
        stacked = jnp.stack(arrays).reshape(len(arrays), rows, spread, heads_here, HEAD)
        return stacked.transpose(2, 3, 0, 1, 4)

    def unpack(packed):
        kinds = packed.shape[2]
        full = packed.transpose(2, 3, 0, 1, 4).reshape(kinds, rows, width)
        return [full[i] for i in range(kinds)]

    local_blocks = blocks // groups
    first = (group * local_blocks).astype(jnp.int32).reshape(1)
    local = exchange(pack([queries, keys, values, cotangent]))
    outs = []
    for h in range(heads_here):
        mine = local[:, h]
        if groups == 1:
            outs.append(attention(partner, first, mine, None, local_blocks)[0])
        else:
            far = lax.all_gather(
                mine[:, 1:3], "ctx", axis=0, tiled=True, axis_index_groups=across
            )
            out, grad_k, grad_v = attention(partner, first, mine, far, local_blocks)
            grads = lax.psum_scatter(
                jnp.stack([grad_k, grad_v], axis=1),
                "ctx",
                scatter_dimension=0,
                tiled=True,
                axis_index_groups=across,
            ).astype(jnp.bfloat16)
            grads = grads.transpose(0, 2, 1, 3).reshape(spread, rows, 2, HEAD).transpose(0, 2, 1, 3)
            outs.append(jnp.concatenate([out, grads], axis=1))
    return tuple(unpack(exchange(jnp.stack(outs, axis=1))))


def call(kernel, place, arrays, out_shape, scratch=(), flops=0, exps=0):
    smem = pl.BlockSpec(memory_space=pltpu.SMEM)
    vmem = pl.BlockSpec(memory_space=pltpu.VMEM)
    moved = sum(a.size * a.dtype.itemsize for a in arrays)
    moved += sum(a.size * a.dtype.itemsize for a in out_shape)
    return pl.pallas_call(
        kernel,
        out_shape=out_shape,
        in_specs=[smem] * len(place) + [vmem] * len(arrays),

        out_specs=[vmem] * len(out_shape),
        scratch_shapes=list(scratch),
        compiler_params=pltpu.CompilerParams(vmem_limit_bytes=40 * 1024 * 1024),
        cost_estimate=pl.CostEstimate(flops=flops, bytes_accessed=moved, transcendentals=exps),
    )(*place, *arrays)


def own_columns(place, arrays, chips):
    count = len(arrays)
    rows = arrays[0].shape[0]

    def kernel(where, *refs):
        out, sems = refs[count:]
        copies = []
        for k in range(chips):
            column = pl.ds(pl.multiple_of(((where[0] ^ k) * 2 + where[1]) * HEAD, HEAD), HEAD)
            for i in range(count):
                copies.append(
                    pltpu.make_async_copy(refs[i].at[:, column], out.at[k, i], sems.at[k, i])
                )
        for copy in copies:
            copy.start()
        for copy in copies:
            copy.wait()

    return pl.pallas_call(
        kernel,
        out_shape=jax.ShapeDtypeStruct((chips, count, rows, HEAD), jnp.bfloat16),
        in_specs=[pl.BlockSpec(memory_space=pltpu.SMEM)] + [pl.BlockSpec(memory_space=pltpu.HBM)] * count,
        out_specs=pl.BlockSpec(memory_space=pltpu.VMEM),
        scratch_shapes=[pltpu.SemaphoreType.DMA((chips, count))],
        compiler_params=pltpu.CompilerParams(vmem_limit_bytes=40 * 1024 * 1024),
    )(place, *[pltpu.with_memory_space_constraint(a, pltpu.HBM) for a in arrays])


def own_rows(place, k, arrays):
    count = len(arrays)
    rows = arrays[0].shape[0]
    span = 2 * HEAD

    def kernel(where, *refs):
        out, sems = refs[count:]
        column = pl.ds(pl.multiple_of((where[0] ^ k) * span, span), span)
        copies = [
            pltpu.make_async_copy(refs[i].at[:, column], out.at[i], sems.at[i])
            for i in range(count)
        ]
        for copy in copies:
            copy.start()
        for copy in copies:
            copy.wait()

    return pl.pallas_call(
        kernel,
        out_shape=jax.ShapeDtypeStruct((count, rows, span), jnp.bfloat16),
        in_specs=[pl.BlockSpec(memory_space=pltpu.SMEM)]
        + [pl.BlockSpec(memory_space=pltpu.HBM)] * count,
        out_specs=pl.BlockSpec(memory_space=pltpu.VMEM),
        scratch_shapes=[pltpu.SemaphoreType.DMA((count,))],
        compiler_params=pltpu.CompilerParams(vmem_limit_bytes=40 * 1024 * 1024),
    )(place, *[pltpu.with_memory_space_constraint(a, pltpu.HBM) for a in arrays])


def other_head(place, piece):
    count, rows, _ = piece.shape

    def kernel(where, piece, out):
        out[...] = piece[:, :, pl.ds(pl.multiple_of((1 - where[1]) * HEAD, HEAD), HEAD)]

    out = jax.ShapeDtypeStruct((count, rows, HEAD), jnp.bfloat16)
    return call(kernel, [place], [piece], [out])[0]


def pack(place, ks, keeps, theirs):
    rows = keeps[0].shape[2]
    count = len(theirs)

    def kernel(where, *refs):
        here, there = halves(where, rows)
        keep = [(ref, i) for ref in refs[: len(keeps)] for i in range(ref.shape[1])]
        theirs = refs[len(keeps) : len(keeps) + count]
        for n, k in enumerate(ks):
            column = pl.ds(pl.multiple_of(((where[0] ^ k) * 2 + where[1]) * HEAD, HEAD), HEAD)
            out = refs[len(keeps) + count + n]
            for i, (ref, j) in enumerate(keep):
                out[i, here] = ref[k, j]
                out[i, there] = theirs[i][:, column]

    piece = jax.ShapeDtypeStruct((count, 2 * rows, HEAD), jnp.bfloat16)
    pieces = call(kernel, [place], [*keeps, *theirs], [piece] * len(ks))
    return dict(zip(ks, pieces))


def cut(place, pieces, bases, count):
    number = len(pieces)
    size = pieces[0].shape[1]

    def kernel(where, *refs):
        there = halves(where, size // 2)[1]
        for n in range(number):
            refs[number][n] = refs[n][bases[n] : bases[n] + count, there]

    out = jax.ShapeDtypeStruct((number, count, size // 2, HEAD), jnp.bfloat16)
    return call(kernel, [place], pieces, [out])[0]


def scatter(place, ks, arrays, picks, other, results, width):
    count = len(picks)
    rows = arrays[0].shape[-2] if other else arrays[0].shape[-2] // 2
    total = len(ks) * count

    def kernel(where, *refs):
        core = where[1]
        half = halves(where, rows)[0]
        outs, sems = refs[-1 - count : -1], refs[-1]
        copies = []
        for n, k in enumerate(ks):
            head = (where[0] ^ k) * 2 + (1 - core if other else core)
            column = pl.ds(pl.multiple_of(head * HEAD, HEAD), HEAD)
            for i in range(count):
                array, index = picks[i][n]
                source = refs[array].at[index] if other else refs[array].at[index, half]
                copies.append(
                    pltpu.make_async_copy(source, outs[i].at[:, column], sems.at[n * count + i])
                )
        for copy in copies:
            copy.start()
        for copy in copies:
            copy.wait()

    smem = pl.BlockSpec(memory_space=pltpu.SMEM)
    vmem = pl.BlockSpec(memory_space=pltpu.VMEM)
    hbm = pl.BlockSpec(memory_space=pltpu.HBM)
    out = jax.ShapeDtypeStruct((rows, width), jnp.bfloat16)
    moved = 2 * count * len(ks) * rows * HEAD * 2
    return pl.pallas_call(
        kernel,
        out_shape=[out] * count,
        in_specs=[smem] + [vmem] * len(arrays) + [hbm] * len(results),
        out_specs=[hbm] * count,
        scratch_shapes=[pltpu.SemaphoreType.DMA((total,))],
        input_output_aliases={1 + len(arrays) + i: i for i in range(len(results))},
        compiler_params=pltpu.CompilerParams(vmem_limit_bytes=40 * 1024 * 1024),
        cost_estimate=pl.CostEstimate(flops=0, bytes_accessed=moved, transcendentals=0),
    )(place, *arrays, *results)


def unpack(place, ks, third, fourth, bases, got_attended, got_grads):
    width = len(ks) * 2 * HEAD
    chips = range(len(ks))
    picks = [[(n, bases[n]) for n in chips]]
    picks += [[(len(ks) + n, i) for n in chips] for i in range(3)]
    outs = scatter(place, ks, [*third, *fourth], picks, False, [], width)
    picks = [[(0, (n, 0)) for n in chips]]
    picks += [[(1, (n, i)) for n in chips] for i in range(3)]
    return scatter(place, ks, [got_attended, got_grads], picks, True, outs, width)


def halves(where, rows):
    core = where[1]
    here = pl.ds(pl.multiple_of(core * rows, rows), rows)
    there = pl.ds(pl.multiple_of((1 - core) * rows, rows), rows)
    return here, there


def forward(place, partner, ks, far, early, pieces):
    chips = len(pieces) + 1
    size = pieces[0].shape[1]

    def kernel(where, partner, mine, theirs, *refs):
        outs = refs[len(pieces) : -2]
        held, weights = refs[-2:]
        here, there = halves(where, size // 2)
        column = pl.ds(pl.multiple_of(where[1] * HEAD, HEAD), HEAD)
        for i in range(3):
            held[where[0] ^ far[0], i, here] = mine[i, :, column]
            held[where[0] ^ far[0], i, there] = theirs[i]
        for n, k in enumerate(ks):
            b = where[0] ^ k
            held[b, :3] = refs[n][:3]
            if k not in far:
                held[b, 4] = refs[n][3]
        for k in range(chips):
            b = where[0] ^ k
            p = partner[b]
            q = held[b, 0]
            s = mm(q, held[b, 1], NT) * SCALE
            t = mm(q, held[p, 1], NT) * SCALE
            peak = jnp.max(jnp.maximum(s, t), axis=1, keepdims=True)
            s, t = jnp.exp(s - peak), jnp.exp(t - peak)
            inverse = 1.0 / jnp.sum(s + t, axis=1, keepdims=True)
            s, t = s * inverse, t * inverse
            weights[b, 0] = s
            weights[b, 1] = t
            attended = mm(s.astype(jnp.bfloat16), held[b, 2], NN)
            attended += mm(t.astype(jnp.bfloat16), held[p, 2], NN)
            attended = attended.astype(jnp.bfloat16)
            held[b, 3] = attended
            if k in far:
                outs[far.index(k)][0] = attended

    out_shape = [
        *[jax.ShapeDtypeStruct((1, size, HEAD), jnp.bfloat16)] * len(far),
        jax.ShapeDtypeStruct((chips, 5, size, HEAD), jnp.bfloat16),
        jax.ShapeDtypeStruct((chips, 2, size, size), jnp.float32),
    ]
    flops = chips * 8 * size * size * HEAD
    exps = chips * 2 * size * size
    outs = call(kernel, [place, partner], [*early, *pieces], out_shape, (), flops, exps)
    return dict(zip(far, outs)), outs[-2], outs[-1]


def backward(place, partner, far, pieces, held, weights):
    chips, _, size, _ = held.shape

    def kernel(where, partner, *refs):
        ins = refs[: len(far)]
        held, weights = refs[len(far) : len(far) + 2]
        outs = refs[len(far) + 2 : len(far) + 2 + chips]
        acc_k, acc_v = refs[len(far) + 2 + chips :]
        acc_k[...] = jnp.zeros_like(acc_k)
        acc_v[...] = jnp.zeros_like(acc_v)
        for k in range(chips):
            b = where[0] ^ k
            q = held[b, 0]
            do = ins[far.index(k)][0] if k in far else held[b, 4]
            delta = jnp.sum(
                do.astype(jnp.float32) * held[b, 3].astype(jnp.float32), axis=1, keepdims=True
            )
            total = None
            for side, c in enumerate((b, partner[b])):
                w = weights[b, side]
                g = (w * (mm(do, held[c, 2], NT) - delta)).astype(jnp.bfloat16)
                term = mm(g, held[c, 1], NN)
                total = term if side == 0 else total + term
                acc_k[c] += mm(g, q, TN)
                acc_v[c] += mm(w.astype(jnp.bfloat16), do, TN)
            outs[k][0] = (SCALE * total).astype(jnp.bfloat16)
        for k in range(chips):
            b = where[0] ^ k
            outs[k][1] = (SCALE * acc_k[b]).astype(jnp.bfloat16)
            outs[k][2] = acc_v[b].astype(jnp.bfloat16)
            if k not in far:
                outs[k][3] = held[b, 3]

    out_shape = [
        jax.ShapeDtypeStruct((3 if k in far else 4, size, HEAD), jnp.bfloat16) for k in range(chips)
    ]
    scratch = [pltpu.VMEM((chips, size, HEAD), jnp.float32)] * 2
    flops = chips * 16 * size * size * HEAD
    outs = call(
        kernel, [place, partner], [*pieces, held, weights], out_shape, scratch, flops
    )
    return dict(enumerate(outs))


def after(array, *earlier):
    return lax.optimization_barrier((array, *earlier))[0]


def by_permutes(queries, keys, values, cotangent, partner):
    devices = lax.axis_size("ctx")
    chips = devices // 2
    me = lax.axis_index("ctx")
    place = jnp.stack([me // 2, me % 2]).astype(jnp.int32)

    def hop(piece, distance):
        return lax.ppermute(piece, "ctx", [(i, i ^ distance) for i in range(devices)])

    far = list(range(chips // 2, chips))
    near = list(range(1, chips // 2))
    ks = [0, *near[:1], *far[:2], *near[1:2], *far[2:3], *near[2:], *far[3:]]

    def to_chips(pieces, ks):
        return {k: hop(pieces[k], 2 * k) for k in ks}

    def in_order(arrived):
        return [arrived[k] for k in ks]

    ins = [queries, keys, values]
    theirs = [hop(a, 1) for a in ins]
    early = own_rows(place, far[0], ins)
    keep = own_columns(after(place, early), ins, chips)
    one = pack(place, far[1:], [keep], theirs)
    their_do = hop(cotangent, 1)
    keep_do = own_columns(place, [cotangent], chips)
    one |= pack(place, [0, *near], [keep, keep_do], [*theirs, their_do])
    first = {0: one[0]} | to_chips(one, far[1:] + near)
    two = pack(after(place, *(first[k] for k in near[:2])), far, [keep_do], [their_do])
    second = to_chips(two, far)
    early = hop(early, 2 * far[0])
    early = [early, hop(other_head(after(place, first[far[2]]), early), 1)]
    later = [k for k in ks if k != far[0]]
    first = [first[k] for k in later]
    three, held, weights = forward(place, partner, later, far, early, first)
    third = {k: hop(after(three[k], second[k]), 2 * k) for k in far}
    four = backward(place, partner, far, [second[k] for k in far], held, weights)
    done = [third[k] for k in far]
    fourth = {0: four[0]} | {k: hop(after(four[k], *done), 2 * k) for k in far + near}
    third |= {k: fourth[k] for k in [0, *near]}
    bases = [0 if k in far else 3 for k in ks]
    third = in_order(third)
    third[0] = after(third[0], *(fourth[k] for k in far[:3]))
    got_attended = hop(cut(place, third, bases, 1), 1)
    fourth = in_order(fourth)
    got_grads = hop(cut(place, fourth, [0] * chips, 3), 1)
    return tuple(unpack(place, ks, third, fourth, bases, got_attended, got_grads))


def body(queries, keys, values, cotangent, partner):
    rows, width = queries.shape
    devices = lax.axis_size("ctx")
    blocks = partner.shape[0]
    in_pairs = devices == 2 * blocks and devices * HEAD == width
    if in_pairs and blocks & (blocks - 1) == 0:
        return by_permutes(queries, keys, values, cotangent, partner)
    return by_all_to_all(queries, keys, values, cotangent, partner)


def solution(mesh):
    split = P(("dp", "ctx"), None)
    return jax.shard_map(
        body,
        mesh=mesh,
        in_specs=(split, split, split, split, P("dp")),
        out_specs=(split, split, split, split),
        check_vma=False,
    )
```
